256 devices in a mesh: ep: 32 (over z, y), tp: 8 (over x, core).
Axes of the slice: x: 4, y: 4, z: 8, core: 2. Of those that a mesh axis runs over, the one named last changes fastest.
Arguments:
- tokens: bfloat16 [8192, 3584], P('ep'), may hold values from -6 to 6
- expert_ids: int32 [8192, 2], P('ep'), may hold values from 0 to 63, as said below
- routing_weights: float32 [8192, 2], P('ep'), may hold values from 0.2 to 1
- up_weight: bfloat16 [64, 3584, 3072], P('ep', None, 'tp'), may hold values from -0.09375 to 0.09375
- down_weight: bfloat16 [64, 3072, 3584], P('ep', 'tp'), may hold values from -0.109375 to 0.109375
Outputs:
- moe_output: bfloat16 [8192, 3584], P('ep', 'tp')
The draws below stay inside these ranges and needn't reach their ends.
Inputs may be any that keep to these rules, and one draw needn't show every extreme that they name: `expert_ids`: A row names two different experts. Among the 256 rows of one ep index no expert is named by more than 10 rows, and one expert, the same for every ep index, is named by exactly 10 rows of every ep index.
All inputs are finite; a program needn't handle non-finite values.
Results may differ from the reference program's by a relative error of at most 0.019.
Values may be sent and summed in bfloat16 or wider, within the bound.
A program may use at most 128 MiB of HBM per device.

```python
import jax
import jax.numpy as jnp
from jax import lax

D = 3584
HID = 3072
TOP = 2
TOK_DEV = 256
EXPERTS = 64
CAP = 10
SLOTS = 320
TOKENS = 8192
N_EP = 32
N_TP = 8


def draw_expert_ids(key, part):
    key = jax.random.fold_in(key, 11)
    block_count = TOKENS // TOK_DEV
    favored = jax.random.randint(jax.random.fold_in(key, 1), (), 0, EXPERTS, dtype=jnp.int32)

    def one_block(block_key):
        first_key, second_key = jax.random.split(block_key)
        others = jax.random.permutation(first_key, EXPERTS - 1).astype(jnp.int32)
        others = others + (others >= favored).astype(jnp.int32)
        sequence = others[jnp.arange(2 * TOK_DEV, dtype=jnp.int32) // CAP]
        leading = sequence[:TOK_DEV]
        trailing = sequence[TOK_DEV:]
        row_number = jnp.arange(TOK_DEV, dtype=jnp.int32)
        leading = jnp.where(row_number < CAP, favored, leading)
        table = jnp.stack([leading, trailing], axis=1)
        order = jax.random.permutation(second_key, TOK_DEV).astype(jnp.int32)
        return table[order]
    block_keys = jax.random.split(jax.random.fold_in(key, 2), block_count)
    return jax.vmap(one_block)(block_keys).reshape(TOKENS, TOP).astype(jnp.int32)


def shard_levels(rng, shape, cuts, smallest, top_value):
    gain, own = 1.0, jax.random.fold_in(rng, 6)
    for axis_at, parts in cuts:
        steps = jnp.exp(jax.random.uniform(jax.random.fold_in(own, axis_at), (parts,), jnp.float32, smallest / len(cuts), top_value / len(cuts)))
        gain = gain * jnp.repeat(steps, shape[axis_at] // parts).reshape([-1 if axis == axis_at else 1 for axis in range(len(shape))])
    return gain


def normal_values(key, extent, width, limit, shards=(), kind=jnp.bfloat16):
    drawn = jax.random.normal(key, extent, jnp.float32) * width
    if len(shards) > 0:
        drawn = shard_levels(key, extent, shards, -0.22, 0.18) * drawn
    return jnp.clip(drawn, min=-limit, max=limit).astype(kind)


def setup_inputs(seed: int = 0) -> dict:
    seeds = jax.random.split(jax.random.key(seed), 6)
    tokens = normal_values(seeds[0], (TOKENS, D), 1.0, 6.0, ((0, 32),))
    expert_ids = draw_expert_ids(jax.random.fold_in(seeds[5], 71), 0)
    routing_weights = jnp.clip(0.2 + 0.8 * jax.random.uniform(seeds[2], (TOKENS, TOP), jnp.float32) ** shard_levels(seeds[2], (TOKENS, TOP), ((0, 32),), -0.2, 0.2), 0.2, 1.0)
    up_weight = normal_values(seeds[3], (EXPERTS, D, HID), D ** -0.5, 0.09375, ((0, 32), (2, 8)))
    down_weight = normal_values(seeds[4], (EXPERTS, HID, D), HID ** -0.5, 0.109375, ((0, 32), (1, 8)))
    return dict(tokens=tokens, expert_ids=expert_ids, routing_weights=routing_weights, up_weight=up_weight, down_weight=down_weight)


def reference(tokens, expert_ids, routing_weights, up_weight, down_weight):
    device_count = N_EP
    flat_ids = expert_ids.reshape(device_count, TOK_DEV * TOP)
    one_hot = (flat_ids[:, :, None] == jnp.arange(EXPERTS, dtype=jnp.int32)[None, None, :]).astype(jnp.int32)
    earlier = jnp.cumsum(one_hot, axis=1) - one_hot
    within = jnp.sum(earlier * one_hot, axis=2).astype(jnp.int32)
    slot_of = (jnp.arange(device_count, dtype=jnp.int32)[:, None] * CAP + within).reshape(TOKENS, TOP).astype(jnp.int32)
    owners = jnp.full((EXPERTS, SLOTS), TOKENS, jnp.int32)
    sources = jnp.repeat(jnp.arange(TOKENS, dtype=jnp.int32), TOP)
    owners = owners.at[expert_ids.reshape(-1), slot_of.reshape(-1)].set(sources)
    padded = jnp.concatenate([tokens, jnp.zeros((1, D), tokens.dtype)], 0)
    unit_count = HID // N_TP

    def expert_apply(operands):
        row_index, up_block, down_block = operands
        routed = padded[row_index]
        summed = jnp.zeros((SLOTS, D), jnp.float32)
        for part_index in range(N_TP):
            first_unit = part_index * unit_count
            raised = jnp.dot(routed, up_block[:, first_unit:first_unit + unit_count], preferred_element_type=jnp.float32)
            hidden = jax.nn.silu(raised).astype(jnp.bfloat16)
            partial_out = jnp.dot(hidden, down_block[first_unit:first_unit + unit_count], preferred_element_type=jnp.float32).astype(jnp.bfloat16)
            summed = summed + partial_out.astype(jnp.float32)
        return summed.astype(jnp.bfloat16)

    expert_out = lax.map(expert_apply, (owners, up_weight, down_weight))
    picked = expert_out[expert_ids, slot_of].astype(jnp.float32)
    mixed = jnp.sum(routing_weights[:, :, None] * picked, axis=1)
    return mixed.astype(jnp.bfloat16)
```

```python
import jax
import jax.numpy as jnp
from jax import lax
from jax.sharding import PartitionSpec as P

TOP = 2


def on_device(tokens, expert_ids, routing_weights, up_weight, down_weight):
    tok_count, width_d = tokens.shape
    local_experts = up_weight.shape[0]
    ep_count = lax.axis_size("ep")
    tp_count = lax.axis_size("tp")
    tp_at = lax.axis_index("tp")
    part_d = width_d // tp_count
    expert_total = local_experts * ep_count
    capacity = 5 * tok_count * TOP // (4 * expert_total)
    rows = expert_total * capacity
    assign = expert_ids.reshape(-1)
    one_hot = (assign[:, None] == jnp.arange(expert_total, dtype=jnp.int32)[None, :]).astype(
        jnp.int32
    )
    earlier = jnp.cumsum(one_hot, axis=0) - one_hot
    within = jnp.sum(earlier * one_hot, axis=1)
    position = (assign * capacity + within).reshape(tok_count, TOP)
    row_at = jnp.arange(rows, dtype=jnp.int32)
    place0 = position[:, 0][:, None] == row_at[None, :]
    place1 = position[:, 1][:, None] == row_at[None, :]
    sent = (place0 | place1).astype(jnp.bfloat16)
    block = lax.dynamic_slice_in_dim(tokens, tp_at * part_d, part_d, 1)
    outgoing = jnp.einsum(
        "tr,td->rd", sent, block, preferred_element_type=jnp.float32
    ).astype(jnp.bfloat16)
    outgoing = outgoing.reshape(ep_count, local_experts * capacity, part_d)
    arrived = lax.all_to_all(outgoing, "ep", split_axis=0, concat_axis=0, tiled=True)
    full = lax.all_gather(arrived, "tp", axis=0, tiled=False)
    full = full.reshape(tp_count, ep_count, local_experts, capacity, part_d)
    up = up_weight.reshape(local_experts, tp_count, part_d, up_weight.shape[2])
    raised = jnp.einsum("srekd,esdh->erkh", full, up, preferred_element_type=jnp.float32)
    hidden = jax.nn.silu(raised).astype(jnp.bfloat16)
    down = down_weight.reshape(local_experts, down_weight.shape[1], tp_count, part_d)
    partial_rows = jnp.einsum(
        "erkh,ehsd->srekd", hidden, down, preferred_element_type=jnp.float32
    ).astype(jnp.bfloat16)
    partial_rows = partial_rows.reshape(tp_count, rows, part_d)
    summed = lax.psum_scatter(partial_rows, "tp", scatter_dimension=0, tiled=False)
    returned = lax.all_to_all(
        summed.reshape(ep_count, local_experts * capacity, part_d),
        "ep",
        split_axis=0,
        concat_axis=0,
        tiled=True,
    ).reshape(rows, part_d)
    first = jnp.dot(place0.astype(jnp.bfloat16), returned, preferred_element_type=jnp.float32)
    second = jnp.dot(place1.astype(jnp.bfloat16), returned, preferred_element_type=jnp.float32)
    mixed = routing_weights[:, :1] * first + routing_weights[:, 1:] * second
    return mixed.astype(jnp.bfloat16)


def solution(mesh):
    placed = (P("ep", None), P("ep", None), P("ep", None), P("ep", None, "tp"), P("ep", "tp", None))
    return jax.shard_map(
        on_device, mesh=mesh, in_specs=placed, out_specs=P("ep", "tp"), check_vma=False
    )
```

```python
import jax
import jax.numpy as jnp
from jax import lax
from jax.experimental import pallas as pl
from jax.experimental.pallas import tpu as pltpu
from jax.sharding import PartitionSpec as P

MESH = pl.DeviceIdType.MESH
BF16 = jnp.bfloat16
F32 = jnp.float32

NZ, NY, NX, NC = 8, 4, 4, 2
TOP = 2
LOCAL = 2
CAP = 10
LANES = 128
TILES = 7
FIRST = 4
BLOCKS = 8
BROWS = 80
ROWS = BLOCKS * BROWS
HALF = BLOCKS // 2
OPP, RIGHT, LEFT, OWN = 0, 1, 2, 3


def kernel(
    ids_ref, rw_ref, tok_hbm, up_hbm, down_hbm, out_ref,
    tok, up, down, place, perm, mixw,
    gz, zb, yb, xb, raised, hid,
    part, other, cross, half_in, full_in, summed, yr, zo, zr, mid_in, mid_out,
    tok_sem, w_sem,
    zs, zr_sem, ys, yr_sem, xs, xr, cs, cr,
    rcs, rcr, rxs, rxr, rys, ryr, rzs, rzr, ms, mr,
):
    ep = lax.axis_index("ep")
    tp = lax.axis_index("tp")
    z, y = lax.div(ep, NY), lax.rem(ep, NY)
    x, c = lax.div(tp, NC), lax.rem(tp, NC)
    right, left, opp = lax.rem(x + 1, NX), lax.rem(x + 3, NX), lax.rem(x + 2, NX)
    twin = x * NC + (1 - c)
    right_id, left_id = right * NC + c, left * NC + c

    def tile(chip, j, core):
        return chip * TILES + core * FIRST + j

    def lanes(g):
        return pl.ds(pl.multiple_of(g * LANES, LANES), LANES)

    def push(src, dst, send, recv, to_ep, to_tp):
        return pltpu.make_async_remote_copy(
            src_ref=src, dst_ref=dst, send_sem=send, recv_sem=recv,
            device_id=(to_ep, to_tp), device_id_type=MESH,
        )

    def owned(j, body):
        if j < FIRST - 1:
            body()
        else:
            pl.when(c == 0)(body)

    barrier = pltpu.get_barrier_semaphore()

    def greet(to_ep, to_tp):
        pl.semaphore_signal(barrier, inc=1, device_id=(to_ep, to_tp), device_id_type=MESH)

    def greet_z(d, _):
        greet(lax.rem(z + d, NZ) * NY + y, tp)
        return 0

    def greet_y(d, _):
        greet(z * NY + lax.rem(y + d, NY), tp)
        return 0

    lax.fori_loop(1, NZ, greet_z, 0)
    lax.fori_loop(1, NY, greet_y, 0)
    greet(ep, right_id)
    greet(ep, left_id)
    greet(ep, twin)

    def tok_copy(j):
        return pltpu.make_async_copy(tok_hbm.at[:, lanes(tile(x, j, c))], tok.at[j], tok_sem.at[j])

    for j in range(FIRST):
        owned(j, lambda j=j: tok_copy(j).start())
    up_copy = pltpu.make_async_copy(up_hbm, up, w_sem.at[0])
    down_copy = pltpu.make_async_copy(down_hbm, down, w_sem.at[1])
    up_copy.start()
    down_copy.start()

    tokens = ids_ref.shape[1]
    experts = LOCAL * NZ * NY
    ids0, ids1 = ids_ref[0:1, :], ids_ref[1:2, :]
    named = lax.broadcasted_iota(jnp.int32, (experts, tokens), 0)
    hot0 = (named == ids0).astype(F32)
    hot1 = (named == ids1).astype(F32)
    before = (
        lax.broadcasted_iota(jnp.int32, (tokens, tokens), 0)
        < lax.broadcasted_iota(jnp.int32, (tokens, tokens), 1)
    ).astype(F32).astype(BF16)
    earlier = jnp.dot((hot0 + hot1).astype(BF16), before, preferred_element_type=F32)
    within0 = jnp.sum(hot0 * earlier, axis=0, keepdims=True).astype(jnp.int32)
    within1 = jnp.sum(hot1 * earlier, axis=0, keepdims=True).astype(jnp.int32)
    pos0 = ids0 * CAP + within0
    pos1 = ids1 * CAP + within1
    for b in range(BLOCKS):
        at = lax.broadcasted_iota(jnp.int32, (BROWS, tokens), 0) + b * BROWS
        hits = jnp.where(at == pos0, 1.0, 0.0) + jnp.where(at == pos1, 1.0, 0.0)
        place[b * BROWS:(b + 1) * BROWS, :] = hits.astype(BF16)

    pl.semaphore_wait(barrier, (NZ - 1) + (NY - 1) + 3)

    def z_copy(src, dst, send, recv, j, d):
        to = lax.rem(z + d, NZ)
        return push(src.at[j, to], dst.at[j, z], send.at[j, d], recv.at[j, d], to * NY + y, tp)

    def z_land(src, dst, send, recv, j, d):
        of = lax.rem(z + NZ - d, NZ)
        return push(src.at[j, of], dst.at[j, of], send.at[j, d], recv.at[j, d], ep, tp)

    def z_start(src, dst, send, recv, j):
        def one(d, _):
            z_copy(src, dst, send, recv, j, d).start()
            return 0

        lax.fori_loop(1, NZ, one, 0)
        dst[j, z] = src[j, z]

    def z_wait(src, dst, send, recv, j):
        def one(d, _):
            z_land(src, dst, send, recv, j, d).wait_recv()
            return 0

        lax.fori_loop(1, NZ, one, 0)

    def z_sent(src, dst, send, recv, j):
        def one(d, _):
            z_copy(src, dst, send, recv, j, d).wait_send()
            return 0

        lax.fori_loop(1, NZ, one, 0)

    def y_rows(at):
        return pl.ds(LOCAL * at, LOCAL)

    def y_copy(src, dst, send, recv, j, g, d):
        to = lax.rem(y + d, NY)
        return push(
            src.at[j, y_rows(to)], dst.at[g, y_rows(y)], send.at[j, d], recv.at[j, d],
            z * NY + to, tp,
        )

    def y_land(src, dst, send, recv, j, g, d):
        of = lax.rem(y + NY - d, NY)
        return push(
            src.at[j, y_rows(of)], dst.at[g, y_rows(of)], send.at[j, d], recv.at[j, d], ep, tp
        )

    def y_start(src, dst, send, recv, j, g):
        def one(d, _):
            y_copy(src, dst, send, recv, j, g, d).start()
            return 0

        lax.fori_loop(1, NY, one, 0)
        dst[g, y_rows(y)] = src[j, y_rows(y)]

    def y_wait(src, dst, send, recv, j, g):
        def one(d, _):
            y_land(src, dst, send, recv, j, g, d).wait_recv()
            return 0

        lax.fori_loop(1, NY, one, 0)

    def y_sent(src, dst, send, recv, j, g):
        def one(d, _):
            y_copy(src, dst, send, recv, j, g, d).wait_send()
            return 0

        lax.fori_loop(1, NY, one, 0)

    def as_blocks(v):
        return v.reshape(BLOCKS, BROWS, LANES)

    def as_rows(v):
        return v.reshape(ROWS, LANES)

    to_z = (gz, zb, zs, zr_sem)
    to_y = (yb, xb, ys, yr_sem)

    def gather(j):
        tok_copy(j).wait()
        rows = jnp.dot(place[...], tok[j], preferred_element_type=F32)
        gz[j] = as_blocks(rows.astype(BF16))
        z_start(*to_z, j)

    def turn(j):
        z_wait(*to_z, j)
        rows = jnp.dot(perm[...], as_rows(zb[j]), preferred_element_type=F32)
        yb[j] = as_blocks(rows.astype(BF16))
        y_start(*to_y, j, tile(x, j, c))

    low, high = pl.ds(0, HALF), pl.ds(HALF, HALF)

    def x_copy(j, kind):
        if kind == 0:
            src, to = xb.at[tile(x, j, c)], right_id
        elif kind == 1:
            src, to = xb.at[tile(x, j, c)], left_id
        elif kind == 2:
            src, to = xb.at[tile(left, j, c), low], right_id
        else:
            src, to = xb.at[tile(right, j, c), high], left_id
        return push(src, src, xs.at[j, kind], xr.at[j, kind], ep, to)

    def x_land(j, kind):
        if kind == 0:
            dst = xb.at[tile(left, j, c)]
        elif kind == 1:
            dst = xb.at[tile(right, j, c)]
        elif kind == 2:
            dst = xb.at[tile(opp, j, c), low]
        else:
            dst = xb.at[tile(opp, j, c), high]
        return push(dst, dst, xs.at[j, kind], xr.at[j, kind], ep, tp)

    chips = {OPP: opp, RIGHT: right, LEFT: left, OWN: x}

    def c_copy(j, kind):
        src = xb.at[tile(chips[kind], j, c)]
        return push(src, src, cs.at[j, kind], cr.at[j, kind], ep, twin)

    def c_land(j, kind):
        dst = xb.at[tile(chips[kind], j, 1 - c)]
        return push(dst, dst, cs.at[j, kind], cr.at[j, kind], ep, tp)

    def spread(j):
        y_wait(*to_y, j, tile(x, j, c))
        x_copy(j, 0).start()
        x_copy(j, 1).start()
        c_copy(j, OWN).start()

    def onward(j):
        x_land(j, 0).wait_recv()
        x_copy(j, 2).start()
        x_land(j, 1).wait_recv()
        x_copy(j, 3).start()
        c_copy(j, LEFT).start()
        c_copy(j, RIGHT).start()

    def last_hop(j):
        x_land(j, 2).wait_recv()
        x_land(j, 3).wait_recv()
        c_copy(j, OPP).start()

    def multiply(j):
        def landed():
            for kind in (OWN, LEFT, RIGHT, OPP):
                c_land(j, kind).wait_recv()

        if j < FIRST - 1:
            landed()
        else:
            pl.when(c == 1)(landed)
        tiles = [chip * TILES + j for chip in range(NX)]
        if j < FIRST - 1:
            tiles += [chip * TILES + FIRST + j for chip in range(NX)]
        for e in range(LOCAL):
            rows = jnp.concatenate(
                [
                    jnp.concatenate([xb[g, LOCAL * at + e] for at in range(NY)], axis=0)
                    for g in tiles
                ],
                axis=1,
            )
            weight = jnp.concatenate([up[e, g * LANES:(g + 1) * LANES, :] for g in tiles], axis=0)
            product = jnp.dot(rows, weight, preferred_element_type=F32)
            if j == 0:
                raised[e] = product
            elif j < FIRST - 1:
                raised[e] = raised[e] + product
            else:
                v = raised[e] + product
                hid[e] = (v / (1.0 + jnp.exp(-v))).astype(BF16)

    for j in range(FIRST):
        owned(j, lambda j=j: gather(j))

    for b in range(BLOCKS):
        row = lax.broadcasted_iota(jnp.int32, (BROWS, 1), 0) + b * BROWS
        block = lax.shift_right_logical(row * 205, 11)
        source = (
            (lax.bitwise_and(block, 7) * BLOCKS + lax.shift_right_logical(block, 3)) * CAP
            + row - block * CAP
        )
        column = lax.broadcasted_iota(jnp.int32, (BROWS, ROWS), 1)
        perm[b * BROWS:(b + 1) * BROWS, :] = jnp.where(column == source, 1.0, 0.0).astype(BF16)

    def do(step, j):
        owned(j, lambda: step(j))

    do(turn, 0)
    do(spread, 0)
    do(turn, 1)
    do(spread, 1)
    do(onward, 0)
    do(turn, 2)
    do(spread, 2)
    do(last_hop, 0)
    do(onward, 1)
    do(turn, 3)
    do(spread, 3)

    w0, w1 = rw_ref[0:1, :], rw_ref[1:2, :]
    for b in range(ROWS // LANES):
        at = lax.broadcasted_iota(jnp.int32, (LANES, tokens), 0) + b * LANES
        mix = jnp.where(at == pos0, w0, 0.0) + jnp.where(at == pos1, w1, 0.0)
        turned = jnp.transpose(mix)
        coarse = turned.astype(BF16)
        mixw[0:tokens, b * LANES:(b + 1) * LANES] = coarse
        mixw[tokens:, b * LANES:(b + 1) * LANES] = (turned - coarse.astype(F32)).astype(BF16)

    up_copy.wait()
    do(last_hop, 1)
    do(onward, 2)
    multiply(0)
    do(onward, 3)
    do(last_hop, 2)
    multiply(1)
    do(last_hop, 3)
    multiply(2)
    multiply(3)
    down_copy.wait()

    back_y = (summed, yr, rys, ryr)
    back_z = (zo, zr, rzs, rzr)

    def rc_copy(j, kind):
        return push(other.at[j, kind], cross.at[j, kind], rcs.at[j, kind], rcr.at[j, kind], ep, twin)

    def rx_copy(j, kind):
        if kind == 0:
            src, dst, to = part.at[j, OPP, low], half_in.at[j, 0], right_id
        elif kind == 1:
            src, dst, to = part.at[j, OPP, high], half_in.at[j, 1], left_id
        elif kind == 2:
            src, dst, to = part.at[j, RIGHT], full_in.at[j, 0], right_id
        else:
            src, dst, to = part.at[j, LEFT], full_in.at[j, 1], left_id
        return push(src, dst, rxs.at[j, kind], rxr.at[j, kind], ep, to)

    def rc_land(j, kind):
        dst = cross.at[j, kind]
        return push(dst, dst, rcs.at[j, kind], rcr.at[j, kind], ep, tp)

    def lower(j, kind):
        chip = chips[kind]
        for e in range(LOCAL):
            mine = down[e, :, lanes(tile(chip, j, c if j < FIRST - 1 else 0))]
            if j < FIRST - 1:
                theirs = down[e, :, lanes(tile(chip, j, 1 - c))]
                weight = jnp.concatenate([mine, theirs], axis=1)
            else:
                weight = mine
            product = jnp.dot(hid[e], weight, preferred_element_type=F32).astype(BF16)
            for at in range(NY):
                rows = product[at * BROWS:(at + 1) * BROWS]
                if j < FIRST - 1:
                    part[j, kind, LOCAL * at + e] = rows[:, :LANES]
                    other[j, kind, LOCAL * at + e] = rows[:, LANES:]
                else:
                    part[j, kind, LOCAL * at + e] = rows
        if j < FIRST - 1:
            rc_copy(j, kind).start()
        else:
            pl.when(c == 1)(lambda: extra_copy(kind).start())

    def extra_copy(kind):
        j = FIRST - 1
        return push(part.at[j, kind], cross.at[j, kind], rcs.at[j, kind], rcr.at[j, kind], ep, twin)

    def lower_all(j):
        for kind in (OPP, RIGHT, LEFT, OWN):
            lower(j, kind)

    def wide(v):
        return v.astype(F32)

    def add_opp(j):
        rc_land(j, OPP).wait_recv()
        part[j, OPP] = (wide(part[j, OPP]) + wide(cross[j, OPP])).astype(BF16)
        rx_copy(j, 0).start()
        rx_copy(j, 1).start()

    def add_sides(j):
        for kind, way, near, far in ((RIGHT, 0, low, high), (LEFT, 1, high, low)):
            rc_land(j, kind).wait_recv()
            part[j, kind, far] = (wide(part[j, kind, far]) + wide(cross[j, kind, far])).astype(BF16)
            rx_copy(j, way).wait_recv()
            part[j, kind, near] = (
                wide(part[j, kind, near]) + wide(cross[j, kind, near]) + wide(half_in[j, way])
            ).astype(BF16)
            rx_copy(j, 2 + way).start()

    def add_own(j):
        rc_land(j, OWN).wait_recv()
        rx_copy(j, 2).wait_recv()
        rx_copy(j, 3).wait_recv()
        summed[j] = (
            (wide(part[j, OWN]) + wide(cross[j, OWN]))
            + (wide(full_in[j, 0]) + wide(full_in[j, 1]))
        ).astype(BF16)
        y_start(*back_y, j, j)

    def turn_back(j):
        y_wait(*back_y, j, j)
        rows = jnp.dot(perm[...], as_rows(yr[j]), preferred_element_type=F32)
        zo[j] = as_blocks(rows.astype(BF16))
        z_start(*back_z, j)

    mid_copy = push(mid_out, mid_in, ms, mr, ep, twin)
    middle = LANES // 2

    def mix(j):
        z_wait(*back_z, j)
        both = jnp.dot(mixw[...], as_rows(zr[j]), preferred_element_type=F32)
        result = (both[:tokens] + both[tokens:]).astype(BF16)
        if j == FIRST - 1:
            mid_out[...] = result
            out_ref[:, j * LANES:j * LANES + middle] = result[:, :middle]
            mid_copy.start()
        else:
            def first():
                out_ref[:, j * LANES:(j + 1) * LANES] = result

            def second():
                out_ref[:, middle + j * LANES:middle + (j + 1) * LANES] = result

            pl.when(c == 0)(first)
            pl.when(c == 1)(second)

    order = (3, 0, 1, 2)
    a, b, d, e = order
    lower_all(a)
    do(add_opp, a)
    lower_all(b)
    do(add_sides, a)
    do(add_opp, b)
    lower_all(d)
    do(add_own, a)
    do(add_sides, b)
    do(add_opp, d)
    lower_all(e)
    do(turn_back, a)
    do(add_own, b)
    do(add_sides, d)
    do(add_opp, e)
    do(turn_back, b)
    do(add_own, d)
    do(add_sides, e)
    do(mix, a)
    do(turn_back, d)
    do(mix, b)
    do(add_own, e)
    do(mix, d)
    do(turn_back, e)

    def take_middle():
        mid_copy.wait_recv()
        out_ref[:, 0:middle] = mid_in[:, middle:]

    pl.when(c == 1)(take_middle)
    do(mix, e)

    def all_sent(j):
        z_sent(*to_z, j)
        y_sent(*to_y, j, tile(x, j, c))
        for kind in range(4):
            x_copy(j, kind).wait_send()
            c_copy(j, kind).wait_send()
            rx_copy(j, kind).wait_send()
            if j < FIRST - 1:
                rc_copy(j, kind).wait_send()
        y_sent(*back_y, j, j)
        z_sent(*back_z, j)

    for j in range(FIRST):
        do(all_sent, j)
    pl.when(c == 0)(lambda: mid_copy.wait_send())

    def extras_sent():
        for kind in range(4):
            extra_copy(kind).wait_send()

    pl.when(c == 1)(extras_sent)


def on_device(tokens, expert_ids, routing_weights, up_weight, down_weight):
    count, width = tokens.shape
    hidden = up_weight.shape[2]
    dma = pltpu.SemaphoreType.DMA
    blocks = (BLOCKS, BROWS, LANES)
    any_space = pl.BlockSpec(memory_space=pl.ANY)
    in_vmem = pl.BlockSpec(memory_space=pltpu.VMEM)
    per_z, per_y, by_kind = dma((FIRST, NZ)), dma((FIRST, NY)), dma((FIRST, 4))
    tile_set = pltpu.VMEM((FIRST,) + blocks, BF16)
    kind_set = pltpu.VMEM((FIRST, 4) + blocks, BF16)
    return pl.pallas_call(
        kernel,
        out_shape=jax.ShapeDtypeStruct((count, width // (NX * NC)), BF16),
        in_specs=[in_vmem, in_vmem, any_space, any_space, any_space],
        out_specs=in_vmem,
        scratch_shapes=[
            pltpu.VMEM((FIRST, count, LANES), BF16),
            pltpu.VMEM(up_weight.shape, BF16),
            pltpu.VMEM(down_weight.shape, BF16),
            pltpu.VMEM((ROWS, count), BF16),
            pltpu.VMEM((ROWS, ROWS), BF16),
            pltpu.VMEM((2 * count, ROWS), BF16),
            tile_set,
            tile_set,
            tile_set,
            pltpu.VMEM((NX * TILES,) + blocks, BF16),
            pltpu.VMEM((LOCAL, ROWS // LOCAL, hidden), F32),
            pltpu.VMEM((LOCAL, ROWS // LOCAL, hidden), BF16),
            kind_set,
            pltpu.VMEM((FIRST - 1, 4) + blocks, BF16),
            kind_set,
            pltpu.VMEM((FIRST, 2, HALF, BROWS, LANES), BF16),
            pltpu.VMEM((FIRST, 2) + blocks, BF16),
            tile_set,
            tile_set,
            tile_set,
            tile_set,
            pltpu.VMEM((count, LANES), BF16),
            pltpu.VMEM((count, LANES), BF16),
            dma((FIRST,)),
            dma((2,)),
            per_z, per_z, per_y, per_y, by_kind, by_kind, by_kind, by_kind,
            by_kind, by_kind, by_kind, by_kind, per_y, per_y, per_z, per_z, dma, dma,
        ],
        compiler_params=pltpu.CompilerParams(
            collective_id=0, has_side_effects=True, vmem_limit_bytes=60 * 1024 * 1024
        ),
        cost_estimate=pl.CostEstimate(
            flops=4 * ROWS * width * hidden, bytes_accessed=8 * width * hidden, transcendentals=0
        ),
        name="experts",
    )(expert_ids.T, routing_weights.T, tokens, up_weight, down_weight)


def solution(mesh):
    placed = (P("ep", None), P("ep", None), P("ep", None), P("ep", None, "tp"), P("ep", "tp", None))
    return jax.shard_map(
        on_device, mesh=mesh, in_specs=placed, out_specs=P("ep", "tp"), check_vma=False
    )
```

```python
import jax
import jax.numpy as jnp
from jax import lax
from jax.experimental import pallas as pl
from jax.experimental.pallas import tpu as pltpu
from jax.sharding import PartitionSpec as P

MESH = pl.DeviceIdType.MESH
BF16 = jnp.bfloat16
F32 = jnp.float32

NZ, NY, NX, NC = 8, 4, 4, 2
TOP = 2
LOCAL = 2
CAP = 10
LANES = 128
TILES = 7
FIRST = 4
BLOCKS = 8
BROWS = 80
ROWS = BLOCKS * BROWS
HALF = BLOCKS // 2
OPP, RIGHT, LEFT, OWN = 0, 1, 2, 3
FIRST_UP, LAST_UP = (3, 3), (1, 1)


def kernel(
    ids_hbm, rw_hbm, tok_hbm, up_hbm, down_hbm, out_ref,
    ids_ref, rw_ref, tok, up, down, place, perm, mixw,
    gz, zb, yb, xb, raised, hid,
    part, other, cross, half_in, full_in, summed, yr, zo, zr, mid_in, mid_out,
    tok_sem, w_sem,
    zs, zr_sem, ys, yr_sem, xs, xr, cs, cr,
    rcs, rcr, rxs, rxr, rys, ryr, rzs, rzr, ms, mr,
):
    ep = lax.axis_index("ep")
    tp = lax.axis_index("tp")
    z, y = lax.div(ep, NY), lax.rem(ep, NY)
    x, c = lax.div(tp, NC), lax.rem(tp, NC)
    right, left, opp = lax.rem(x + 1, NX), lax.rem(x + 3, NX), lax.rem(x + 2, NX)
    twin = x * NC + (1 - c)
    right_id, left_id = right * NC + c, left * NC + c

    def tile(chip, j, core):
        return chip * TILES + core * FIRST + j

    def lanes(g):
        return pl.ds(pl.multiple_of(g * LANES, LANES), LANES)

    def push(src, dst, send, recv, to_ep, to_tp):
        return pltpu.make_async_remote_copy(
            src_ref=src, dst_ref=dst, send_sem=send, recv_sem=recv,
            device_id=(to_ep, to_tp), device_id_type=MESH,
        )

    def owned(j, body):
        if j < FIRST - 1:
            body()
        else:
            pl.when(c == 0)(body)

    barrier = pltpu.get_barrier_semaphore()

    def greet(to_ep, to_tp):
        pl.semaphore_signal(barrier, inc=1, device_id=(to_ep, to_tp), device_id_type=MESH)

    def greet_z(d, _):
        greet(lax.rem(z + d, NZ) * NY + y, tp)
        return 0

    def greet_y(d, _):
        greet(z * NY + lax.rem(y + d, NY), tp)
        return 0

    lax.fori_loop(1, NZ, greet_z, 0)
    lax.fori_loop(1, NY, greet_y, 0)
    greet(ep, right_id)
    greet(ep, left_id)
    greet(ep, twin)

    ids_copy = pltpu.make_async_copy(ids_hbm, ids_ref, w_sem.at[2])
    rw_copy = pltpu.make_async_copy(rw_hbm, rw_ref, w_sem.at[3])
    ids_copy.start()
    rw_copy.start()

    def tok_copy(j):
        return pltpu.make_async_copy(tok_hbm.at[:, lanes(tile(x, j, c))], tok.at[j], tok_sem.at[j])

    for j in range(FIRST):
        owned(j, lambda j=j: tok_copy(j).start())
    up_copy = pltpu.make_async_copy(up_hbm, up, w_sem.at[0])
    down_copy = pltpu.make_async_copy(down_hbm, down, w_sem.at[1])
    up_copy.start()
    down_copy.start()

    tokens = ids_ref.shape[1]
    experts = LOCAL * NZ * NY
    ids_copy.wait()
    ids0, ids1 = ids_ref[0:1, :], ids_ref[1:2, :]
    named = lax.broadcasted_iota(jnp.int32, (experts, tokens), 0)
    hot0 = (named == ids0).astype(F32)
    hot1 = (named == ids1).astype(F32)
    before = (
        lax.broadcasted_iota(jnp.int32, (tokens, tokens), 0)
        < lax.broadcasted_iota(jnp.int32, (tokens, tokens), 1)
    ).astype(F32).astype(BF16)
    earlier = jnp.dot((hot0 + hot1).astype(BF16), before, preferred_element_type=F32)
    within0 = jnp.sum(hot0 * earlier, axis=0, keepdims=True).astype(jnp.int32)
    within1 = jnp.sum(hot1 * earlier, axis=0, keepdims=True).astype(jnp.int32)
    pos0 = ids0 * CAP + within0
    pos1 = ids1 * CAP + within1
    for b in range(BLOCKS):
        at = lax.broadcasted_iota(jnp.int32, (BROWS, tokens), 0) + b * BROWS
        hits = jnp.where(at == pos0, 1.0, 0.0) + jnp.where(at == pos1, 1.0, 0.0)
        place[b * BROWS:(b + 1) * BROWS, :] = hits.astype(BF16)

    pl.semaphore_wait(barrier, (NZ - 1) + (NY - 1) + 3)

    def z_copy(src, dst, send, recv, j, d):
        to = lax.rem(z + d, NZ)
        return push(src.at[j, to], dst.at[j, z], send.at[j, d], recv.at[j, d], to * NY + y, tp)

    def z_land(src, dst, send, recv, j, d):
        of = lax.rem(z + NZ - d, NZ)
        return push(src.at[j, of], dst.at[j, of], send.at[j, d], recv.at[j, d], ep, tp)

    def z_start(src, dst, send, recv, j):
        def one(d, _):
            z_copy(src, dst, send, recv, j, d).start()
            return 0

        lax.fori_loop(1, NZ, one, 0)
        dst[j, z] = src[j, z]

    def z_wait(src, dst, send, recv, j):
        def one(d, _):
            z_land(src, dst, send, recv, j, d).wait_recv()
            return 0

        lax.fori_loop(1, NZ, one, 0)

    def z_sent(src, dst, send, recv, j):
        def one(d, _):
            z_copy(src, dst, send, recv, j, d).wait_send()
            return 0

        lax.fori_loop(1, NZ, one, 0)

    def y_rows(at):
        return pl.ds(LOCAL * at, LOCAL)

    def as_blocks(v):
        return v.reshape(BLOCKS, BROWS, LANES)

    def as_rows(v):
        return v.reshape(ROWS, LANES)

    def quarter(q):
        return pl.ds(LOCAL * q, LOCAL)

    def half(h):
        return pl.ds(HALF * h, HALF)

    to_z = (gz, zb, zs, zr_sem)

    def y_copy(j, d):
        to = lax.rem(y + d, NY)
        return push(
            yb.at[j, y_rows(to)], xb.at[tile(x, j, c), quarter(d)], ys.at[j, d], yr_sem.at[j, d],
            z * NY + to, tp,
        )

    def x_copy(j, q, way):
        if way == 0:
            src, to = xb.at[tile(x, j, c), quarter(q)], right_id
        elif way == 1:
            src, to = xb.at[tile(x, j, c), quarter(q)], left_id
        elif q % 2 == 0:
            src, to = xb.at[tile(left, j, c), quarter(q)], right_id
        else:
            src, to = xb.at[tile(right, j, c), quarter(q)], left_id
        return push(src, src, xs.at[j, way * NY + q], xr.at[j, way * NY + q], ep, to)

    def x_land(j, q, way):
        chip = (left, right, opp)[way]
        dst = xb.at[tile(chip, j, c), quarter(q)]
        return push(dst, dst, xs.at[j, way * NY + q], xr.at[j, way * NY + q], ep, tp)

    chips = {OPP: opp, RIGHT: right, LEFT: left, OWN: x}

    def c_copy(j, h, kind):
        src = xb.at[tile(chips[kind], j, c), half(h)]
        return push(src, src, cs.at[j, 4 * h + kind], cr.at[j, 4 * h + kind], ep, twin)

    def c_land(j, h, kind):
        dst = xb.at[tile(chips[kind], j, 1 - c), half(h)]
        return push(dst, dst, cs.at[j, 4 * h + kind], cr.at[j, 4 * h + kind], ep, tp)

    def gather(j):
        tok_copy(j).wait()
        rows = jnp.dot(place[...], tok[j], preferred_element_type=F32)
        gz[j] = as_blocks(rows.astype(BF16))
        z_start(*to_z, j)

    def spread(j, q):
        x_copy(j, q, 0).start()
        x_copy(j, q, 1).start()

    def turn(j):
        z_wait(*to_z, j)
        rows = jnp.dot(perm[...], as_rows(zb[j]), preferred_element_type=F32)
        yb[j] = as_blocks(rows.astype(BF16))
        for d in (2, 1, 3):
            y_copy(j, d).start()
        xb[tile(x, j, c), quarter(0)] = yb[j, y_rows(y)]
        spread(j, 0)

    def side(j, q):
        y_copy(j, q).wait_recv()
        spread(j, q)
        if q < 3:
            c_copy(j, q // 2, OWN).start()

    def forward(j, q):
        x_land(j, q, q % 2).wait_recv()
        x_copy(j, q, 2).start()

    def pass_left(j, h):
        x_land(j, 2 * h + 1, 0).wait_recv()
        c_copy(j, h, LEFT).start()

    def pass_right(j, h):
        x_land(j, 2 * h, 1).wait_recv()
        c_copy(j, h, RIGHT).start()

    def last_hop(j, h):
        x_land(j, 2 * h, 2).wait_recv()
        x_land(j, 2 * h + 1, 2).wait_recv()
        c_copy(j, h, OPP).start()

    def multiply(j, h):
        def landed():
            for kind in (OWN, LEFT, RIGHT, OPP):
                c_land(j, h, kind).wait_recv()

        if j < FIRST - 1:
            landed()
        else:
            pl.when(c == 1)(landed)
        tiles = [chip * TILES + j for chip in range(NX)]
        if j < FIRST - 1:
            tiles += [chip * TILES + FIRST + j for chip in range(NX)]
        for e in range(LOCAL):
            rows = jnp.concatenate(
                [
                    jnp.concatenate([xb[g, LOCAL * q + e] for q in (2 * h, 2 * h + 1)], axis=0)
                    for g in tiles
                ],
                axis=1,
            )
            weight = jnp.concatenate([up[e, g * LANES:(g + 1) * LANES, :] for g in tiles], axis=0)
            product = jnp.dot(rows, weight, preferred_element_type=F32)
            if j == FIRST_UP[h]:
                raised[h, e] = product
            elif j != LAST_UP[h]:
                raised[h, e] = raised[h, e] + product
            else:
                v = raised[h, e] + product
                hid[h, e] = (v / (1.0 + jnp.exp(-v))).astype(BF16)

    def make_perm():
        for b in range(BLOCKS):
            row = lax.broadcasted_iota(jnp.int32, (BROWS, 1), 0) + b * BROWS
            block = lax.shift_right_logical(row * 205, 11)
            source = (
                (lax.bitwise_and(block, 7) * BLOCKS + lax.shift_right_logical(block, 3)) * CAP
                + row - block * CAP
            )
            column = lax.broadcasted_iota(jnp.int32, (BROWS, ROWS), 1)
            perm[b * BROWS:(b + 1) * BROWS, :] = jnp.where(column == source, 1.0, 0.0).astype(BF16)

    def make_mix():
        rw_copy.wait()
        w0, w1 = rw_ref[0:1, :], rw_ref[1:2, :]
        for b in range(BLOCKS):
            at = lax.broadcasted_iota(jnp.int32, (BROWS, tokens), 0) + b * BROWS
            mix = jnp.where(at == pos0, w0, 0.0) + jnp.where(at == pos1, w1, 0.0)
            coarse = mix.astype(BF16)
            mixw[b * BROWS:(b + 1) * BROWS, 0:tokens] = coarse
            mixw[b * BROWS:(b + 1) * BROWS, tokens:] = (mix - coarse.astype(F32)).astype(BF16)

    back_z = (zo, zr, rzs, rzr)

    def rc_copy(j, h, kind):
        src = (other if j < FIRST - 1 else part).at[j, kind, half(h)]
        at = 4 * h + kind
        return push(src, cross.at[j, kind, half(h)], rcs.at[j, at], rcr.at[j, at], ep, twin)

    def rc_land(j, h, kind):
        dst = cross.at[j, kind, half(h)]
        at = 4 * h + kind
        return push(dst, dst, rcs.at[j, at], rcr.at[j, at], ep, tp)

    def rx_copy(j, h, kind):
        if kind == 0:
            src, dst, to = part.at[j, OPP, quarter(2 * h)], half_in.at[j, h, 0], right_id
        elif kind == 1:
            src, dst, to = part.at[j, OPP, quarter(2 * h + 1)], half_in.at[j, h, 1], left_id
        elif kind == 2:
            src, dst, to = part.at[j, RIGHT, half(h)], full_in.at[j, 0, half(h)], right_id
        else:
            src, dst, to = part.at[j, LEFT, half(h)], full_in.at[j, 1, half(h)], left_id
        at = 4 * h + kind
        return push(src, dst, rxs.at[j, at], rxr.at[j, at], ep, to)

    def ry_copy(j, d):
        to = lax.rem(y + NY - d, NY)
        return push(
            summed.at[j, quarter(d)], yr.at[j, y_rows(y)], rys.at[j, d], ryr.at[j, d],
            z * NY + to, tp,
        )

    def ry_land(j, d):
        dst = yr.at[j, y_rows(lax.rem(y + d, NY))]
        return push(dst, dst, rys.at[j, d], ryr.at[j, d], ep, tp)

    def lower(j, h, kind):
        chip = chips[kind]
        for e in range(LOCAL):
            mine = down[e, :, lanes(tile(chip, j, c if j < FIRST - 1 else 0))]
            if j < FIRST - 1:
                theirs = down[e, :, lanes(tile(chip, j, 1 - c))]
                weight = jnp.concatenate([mine, theirs], axis=1)
            else:
                weight = mine
            product = jnp.dot(hid[h, e], weight, preferred_element_type=F32).astype(BF16)
            for i in range(2):
                at = LOCAL * (2 * h + i) + e
                rows = product[i * BROWS:(i + 1) * BROWS]
                if j < FIRST - 1:
                    part[j, kind, at] = rows[:, :LANES]
                    other[j, kind, at] = rows[:, LANES:]
                else:
                    part[j, kind, at] = rows
        if j < FIRST - 1:
            rc_copy(j, h, kind).start()
        else:
            pl.when(c == 1)(lambda: rc_copy(j, h, kind).start())

    def wide(v):
        return v.astype(F32)

    def add_opp(j, h):
        rc_land(j, h, OPP).wait_recv()
        at = half(h)
        part[j, OPP, at] = (wide(part[j, OPP, at]) + wide(cross[j, OPP, at])).astype(BF16)
        rx_copy(j, h, 0).start()
        rx_copy(j, h, 1).start()

    def add_side(j, h, kind):
        way = 0 if kind == RIGHT else 1
        near, far = quarter(2 * h + way), quarter(2 * h + 1 - way)
        rc_land(j, h, kind).wait_recv()
        part[j, kind, far] = (wide(part[j, kind, far]) + wide(cross[j, kind, far])).astype(BF16)
        rx_copy(j, h, way).wait_recv()
        part[j, kind, near] = (
            wide(part[j, kind, near]) + wide(cross[j, kind, near]) + wide(half_in[j, h, way])
        ).astype(BF16)
        rx_copy(j, h, 2 + way).start()

    def add_own(j, h):
        rc_land(j, h, OWN).wait_recv()
        rx_copy(j, h, 2).wait_recv()
        rx_copy(j, h, 3).wait_recv()
        at = half(h)
        summed[j, at] = (
            (wide(part[j, OWN, at]) + wide(cross[j, OWN, at]))
            + (wide(full_in[j, 0, at]) + wide(full_in[j, 1, at]))
        ).astype(BF16)
        if h == 0:
            ry_copy(j, 1).start()
            yr[j, y_rows(y)] = summed[j, quarter(0)]
        else:
            ry_copy(j, 2).start()
            ry_copy(j, 3).start()

    def turn_back(j):
        for d in (1, 2, 3):
            ry_land(j, d).wait_recv()
        rows = jnp.dot(perm[...], as_rows(yr[j]), preferred_element_type=F32)
        zo[j] = as_blocks(rows.astype(BF16))
        z_start(*back_z, j)

    mid_copy = push(mid_out, mid_in, ms, mr, ep, twin)
    middle = LANES // 2

    def mix(j):
        z_wait(*back_z, j)
        both = lax.dot_general(
            as_rows(zr[j]), mixw[...], (((0,), (0,)), ((), ())), preferred_element_type=F32
        )
        result = (both[:, :tokens] + both[:, tokens:]).astype(BF16)
        if j == FIRST - 1:
            out_ref[j * LANES:j * LANES + middle, :] = result[:middle]
            mid_out[...] = result[middle:]
            mid_copy.start()
        else:
            def first():
                out_ref[j * LANES:(j + 1) * LANES, :] = result

            def second():
                out_ref[middle + j * LANES:middle + (j + 1) * LANES, :] = result

            pl.when(c == 0)(first)
            pl.when(c == 1)(second)

    def take_middle():
        mid_copy.wait_recv()
        out_ref[0:middle, :] = mid_in[...]

    def do(step, j, *h):
        owned(j, lambda: step(j, *h))

    do(gather, 3)
    do(gather, 0)
    do(gather, 2)
    do(gather, 1)
    make_perm()
    do(turn, 3)
    do(turn, 0)
    do(side, 3, 3)
    do(side, 3, 1)
    do(side, 3, 2)
    do(turn, 2)
    do(side, 0, 3)
    do(side, 0, 2)
    do(side, 0, 1)
    do(turn, 1)
    do(side, 2, 1)
    do(forward, 0, 0)
    do(side, 2, 3)
    do(forward, 0, 1)
    do(forward, 3, 1)
    do(forward, 3, 0)
    do(pass_left, 0, 0)
    do(side, 2, 2)
    do(side, 1, 1)
    do(pass_left, 3, 0)
    do(side, 1, 3)
    do(forward, 2, 1)
    do(forward, 2, 0)
    do(side, 1, 2)
    do(pass_right, 2, 0)
    do(last_hop, 3, 0)
    do(forward, 1, 0)
    do(forward, 1, 1)
    do(pass_right, 0, 0)
    do(forward, 3, 2)
    do(forward, 3, 3)
    make_mix()
    do(forward, 2, 2)
    do(forward, 2, 3)
    do(pass_left, 2, 0)
    do(pass_right, 3, 0)
    do(forward, 0, 2)
    do(last_hop, 0, 0)
    do(pass_left, 0, 1)
    do(pass_right, 3, 1)
    do(forward, 0, 3)
    do(pass_right, 0, 1)
    do(forward, 1, 3)
    do(pass_left, 3, 1)
    do(pass_left, 1, 0)
    do(pass_right, 1, 0)
    do(pass_left, 2, 1)
    do(last_hop, 2, 0)
    up_copy.wait()
    multiply(3, 0)
    do(forward, 1, 2)
    do(pass_right, 1, 1)
    do(last_hop, 1, 0)
    do(pass_right, 2, 1)
    multiply(0, 0)
    multiply(2, 0)
    do(last_hop, 3, 1)
    do(pass_left, 1, 1)
    multiply(1, 0)
    down_copy.wait()
    lower(3, 0, OPP)
    do(last_hop, 2, 1)
    lower(0, 0, OPP)
    lower(1, 0, OPP)
    lower(2, 0, OPP)
    multiply(3, 1)
    do(last_hop, 0, 1)
    lower(1, 0, RIGHT)
    do(add_opp, 3, 0)
    do(last_hop, 1, 1)
    multiply(2, 1)
    do(add_opp, 1, 0)
    do(add_opp, 0, 0)
    multiply(0, 1)
    multiply(1, 1)
    lower(0, 1, OPP)
    lower(3, 0, RIGHT)
    do(add_opp, 2, 0)
    lower(3, 1, OPP)
    lower(3, 0, LEFT)
    lower(2, 0, LEFT)
    lower(0, 1, LEFT)
    lower(2, 1, OPP)
    do(add_opp, 0, 1)
    lower(1, 1, OWN)
    lower(2, 1, RIGHT)
    lower(0, 0, OWN)
    do(add_side, 3, 0, RIGHT)
    do(add_side, 3, 0, LEFT)
    lower(1, 1, OPP)
    lower(0, 1, RIGHT)
    lower(3, 1, RIGHT)
    do(add_opp, 3, 1)
    lower(0, 0, RIGHT)
    lower(0, 1, OWN)
    lower(2, 1, LEFT)
    do(add_opp, 2, 1)
    lower(0, 0, LEFT)
    lower(1, 1, LEFT)
    lower(3, 1, LEFT)
    lower(3, 0, OWN)
    lower(3, 1, OWN)
    do(add_side, 0, 1, RIGHT)
    do(add_side, 0, 1, LEFT)
    do(add_side, 0, 0, RIGHT)
    do(add_side, 0, 0, LEFT)
    do(add_side, 3, 1, RIGHT)
    do(add_side, 3, 1, LEFT)
    lower(2, 0, RIGHT)
    lower(2, 0, OWN)
    do(add_own, 3, 0)
    do(add_opp, 1, 1)
    lower(2, 1, OWN)
    lower(1, 0, LEFT)
    do(add_own, 0, 1)
    lower(1, 1, RIGHT)
    do(add_side, 2, 1, LEFT)
    do(add_side, 2, 1, RIGHT)
    do(add_side, 2, 0, LEFT)
    do(add_own, 0, 0)
    do(add_side, 2, 0, RIGHT)
    do(add_own, 3, 1)
    do(turn_back, 0)
    do(add_side, 1, 1, LEFT)
    do(add_side, 1, 1, RIGHT)
    do(add_own, 2, 1)
    do(add_side, 1, 0, LEFT)
    lower(1, 0, OWN)
    do(add_side, 1, 0, RIGHT)
    do(add_own, 2, 0)
    do(turn_back, 3)
    do(add_own, 1, 1)
    do(turn_back, 2)
    do(add_own, 1, 0)
    do(mix, 0)
    do(mix, 3)
    do(turn_back, 1)
    do(mix, 2)
    pl.when(c == 1)(take_middle)
    do(mix, 1)

    def all_sent(j):
        z_sent(*to_z, j)
        z_sent(*back_z, j)
        for d in range(1, NY):
            y_copy(j, d).wait_send()
            ry_copy(j, d).wait_send()
        for q in range(NY):
            for way in range(3):
                x_copy(j, q, way).wait_send()
        for h in range(2):
            for kind in range(4):
                c_copy(j, h, kind).wait_send()
                rx_copy(j, h, kind).wait_send()
                if j < FIRST - 1:
                    rc_copy(j, h, kind).wait_send()

    for j in range(FIRST):
        do(all_sent, j)
    pl.when(c == 0)(lambda: mid_copy.wait_send())

    def extras_sent():
        for h in range(2):
            for kind in range(4):
                rc_copy(FIRST - 1, h, kind).wait_send()

    pl.when(c == 1)(extras_sent)


def on_device(tokens, expert_ids, routing_weights, up_weight, down_weight):
    count, width = tokens.shape
    hidden = up_weight.shape[2]
    dma = pltpu.SemaphoreType.DMA
    blocks = (BLOCKS, BROWS, LANES)
    any_space = pl.BlockSpec(memory_space=pl.ANY)
    in_vmem = pl.BlockSpec(memory_space=pltpu.VMEM)
    per_z, per_y = dma((FIRST, NZ)), dma((FIRST, NY))
    by_way, by_kind = dma((FIRST, 3 * NY)), dma((FIRST, 8))
    tile_set = pltpu.VMEM((FIRST,) + blocks, BF16)
    kind_set = pltpu.VMEM((FIRST, 4) + blocks, BF16)
    return pl.pallas_call(
        kernel,
        out_shape=jax.ShapeDtypeStruct((width // (NX * NC), count), BF16),
        in_specs=[any_space] * 5,
        out_specs=in_vmem,
        scratch_shapes=[
            pltpu.VMEM((TOP, count), jnp.int32),
            pltpu.VMEM((TOP, count), F32),
            pltpu.VMEM((FIRST, count, LANES), BF16),
            pltpu.VMEM(up_weight.shape, BF16),
            pltpu.VMEM(down_weight.shape, BF16),
            pltpu.VMEM((ROWS, count), BF16),
            pltpu.VMEM((ROWS, ROWS), BF16),
            pltpu.VMEM((ROWS, 2 * count), BF16),
            tile_set,
            tile_set,
            tile_set,
            pltpu.VMEM((NX * TILES,) + blocks, BF16),
            pltpu.VMEM((2, LOCAL, ROWS // LOCAL // 2, hidden), F32),
            pltpu.VMEM((2, LOCAL, ROWS // LOCAL // 2, hidden), BF16),
            kind_set,
            pltpu.VMEM((FIRST - 1, 4) + blocks, BF16),
            kind_set,
            pltpu.VMEM((FIRST, 2, 2, LOCAL, BROWS, LANES), BF16),
            pltpu.VMEM((FIRST, 2) + blocks, BF16),
            tile_set,
            tile_set,
            tile_set,
            tile_set,
            pltpu.VMEM((LANES // 2, count), BF16),
            pltpu.VMEM((LANES // 2, count), BF16),
            dma((FIRST,)),
            dma((4,)),
            per_z, per_z, per_y, per_y, by_way, by_way, by_kind, by_kind,
            by_kind, by_kind, by_kind, by_kind, per_y, per_y, per_z, per_z, dma, dma,
        ],
        compiler_params=pltpu.CompilerParams(
            collective_id=0, has_side_effects=True, vmem_limit_bytes=52 * 1024 * 1024
        ),
        cost_estimate=pl.CostEstimate(
            flops=4 * ROWS * width * hidden, bytes_accessed=8 * width * hidden, transcendentals=0
        ),
        name="experts",
    )(expert_ids.T, routing_weights.T, tokens, up_weight, down_weight).T


def solution(mesh):
    placed = (P("ep", None), P("ep", None), P("ep", None), P("ep", None, "tp"), P("ep", "tp", None))
    return jax.shard_map(
        on_device, mesh=mesh, in_specs=placed, out_specs=P("ep", "tp"), check_vma=False
    )
```

```python
import jax
import jax.numpy as jnp
from jax import lax
from jax.experimental import pallas as pl
from jax.experimental.pallas import tpu as pltpu
from jax.sharding import PartitionSpec as P

MESH = pl.DeviceIdType.MESH
BF16 = jnp.bfloat16
F32 = jnp.float32

NZ, NY, NX, NC = 8, 4, 4, 2
TOP = 2
LOCAL = 2
CAP = 10
LANES = 128
TILES = 7
FIRST = 4
BLOCKS = 8
BROWS = 80
ROWS = BLOCKS * BROWS
HALF = BLOCKS // 2
OPP, RIGHT, LEFT, OWN = 0, 1, 2, 3
FIRST_OUT = (2, 1)
OVER_Z = (0, 3,)
FIRST_UP, LAST_UP = (2, 2), (0, 1)


def kernel(
    ids_hbm, rw_hbm, tok_hbm, up_hbm, down_hbm, out_ref,
    ids_ref, rw_ref, tok, up, down, place, perm, mixw,
    tok2, gz2, zb2, yb2, gz, zb, yb, xb, raised, hid,
    part, other, cross, half_in, full_in, summed, yr, zo, zr, mid_in, mid_out,
    tok_sem, w_sem,
    tok2_sem, zs2, zr2, ys2, yr2,
    zs, zr_sem, ys, yr_sem, xs, xr, cs, cr,
    rcs, rcr, rxs, rxr, rys, ryr, rzs, rzr, ms, mr,
):
    ep = lax.axis_index("ep")
    tp = lax.axis_index("tp")
    z, y = lax.div(ep, NY), lax.rem(ep, NY)
    x, c = lax.div(tp, NC), lax.rem(tp, NC)
    right, left, opp = lax.rem(x + 1, NX), lax.rem(x + 3, NX), lax.rem(x + 2, NX)
    twin = x * NC + (1 - c)
    right_id, left_id = right * NC + c, left * NC + c

    def tile(chip, j, core):
        return chip * TILES + core * FIRST + j

    def lanes(g):
        return pl.ds(pl.multiple_of(g * LANES, LANES), LANES)

    def push(src, dst, send, recv, to_ep, to_tp):
        return pltpu.make_async_remote_copy(
            src_ref=src, dst_ref=dst, send_sem=send, recv_sem=recv,
            device_id=(to_ep, to_tp), device_id_type=MESH,
        )

    def owned(j, body):
        if j < FIRST - 1:
            body()
        else:
            pl.when(c == 0)(body)

    barrier = pltpu.get_barrier_semaphore()

    def greet(to_ep, to_tp):
        pl.semaphore_signal(barrier, inc=1, device_id=(to_ep, to_tp), device_id_type=MESH)

    def greet_z(d, _):
        greet(lax.rem(z + d, NZ) * NY + y, tp)
        return 0

    def greet_y(d, _):
        greet(z * NY + lax.rem(y + d, NY), tp)
        return 0

    lax.fori_loop(1, NZ, greet_z, 0)
    lax.fori_loop(1, NY, greet_y, 0)
    greet(ep, right_id)
    greet(ep, left_id)
    greet(ep, twin)

    ids_copy = pltpu.make_async_copy(ids_hbm, ids_ref, w_sem.at[2])
    rw_copy = pltpu.make_async_copy(rw_hbm, rw_ref, w_sem.at[3])
    ids_copy.start()
    rw_copy.start()

    def tok_copy(j):
        return pltpu.make_async_copy(tok_hbm.at[:, lanes(tile(x, j, c))], tok.at[j], tok_sem.at[j])

    def tok2_copy(j):
        return pltpu.make_async_copy(
            tok_hbm.at[:, lanes(tile(opp, j, c))], tok2.at[j], tok2_sem.at[j]
        )

    for j in FIRST_OUT + tuple(j for j in range(FIRST) if j not in FIRST_OUT):
        owned(j, lambda j=j: tok_copy(j).start())
    for j in OVER_Z:
        owned(j, lambda j=j: tok2_copy(j).start())
    up_copy = pltpu.make_async_copy(up_hbm, up, w_sem.at[0])
    down_copy = pltpu.make_async_copy(down_hbm, down, w_sem.at[1])
    up_copy.start()
    down_copy.start()

    tokens = ids_ref.shape[1]
    experts = LOCAL * NZ * NY
    ids_copy.wait()
    ids0, ids1 = ids_ref[0:1, :], ids_ref[1:2, :]
    named = lax.broadcasted_iota(jnp.int32, (experts, tokens), 0)
    hot0 = (named == ids0).astype(F32)
    hot1 = (named == ids1).astype(F32)
    before = (
        lax.broadcasted_iota(jnp.int32, (tokens, tokens), 0)
        < lax.broadcasted_iota(jnp.int32, (tokens, tokens), 1)
    ).astype(F32).astype(BF16)
    earlier = jnp.dot((hot0 + hot1).astype(BF16), before, preferred_element_type=F32)
    within0 = jnp.sum(hot0 * earlier, axis=0, keepdims=True).astype(jnp.int32)
    within1 = jnp.sum(hot1 * earlier, axis=0, keepdims=True).astype(jnp.int32)
    pos0 = ids0 * CAP + within0
    pos1 = ids1 * CAP + within1
    for b in range(BLOCKS):
        at = lax.broadcasted_iota(jnp.int32, (BROWS, tokens), 0) + b * BROWS
        hits = jnp.where(at == pos0, 1.0, 0.0) + jnp.where(at == pos1, 1.0, 0.0)
        place[b * BROWS:(b + 1) * BROWS, :] = hits.astype(BF16)

    def fill(j):
        tok_copy(j).wait()
        rows = jnp.dot(place[...], tok[j], preferred_element_type=F32)
        gz[j] = rows.astype(BF16).reshape(BLOCKS, BROWS, LANES)

    for j in FIRST_OUT:
        owned(j, lambda j=j: fill(j))

    pl.semaphore_wait(barrier, (NZ - 1) + (NY - 1) + 3)

    def z_copy(src, dst, send, recv, j, d):
        to = lax.rem(z + d, NZ)
        return push(src.at[j, to], dst.at[j, z], send.at[j, d], recv.at[j, d], to * NY + y, tp)

    def z_land(src, dst, send, recv, j, d):
        of = lax.rem(z + NZ - d, NZ)
        return push(src.at[j, of], dst.at[j, of], send.at[j, d], recv.at[j, d], ep, tp)

    def z_start(src, dst, send, recv, j):
        def one(d, _):
            z_copy(src, dst, send, recv, j, d).start()
            return 0

        lax.fori_loop(1, NZ, one, 0)
        dst[j, z] = src[j, z]

    def z_wait(src, dst, send, recv, j):
        def one(d, _):
            z_land(src, dst, send, recv, j, d).wait_recv()
            return 0

        lax.fori_loop(1, NZ, one, 0)

    def z_sent(src, dst, send, recv, j):
        def one(d, _):
            z_copy(src, dst, send, recv, j, d).wait_send()
            return 0

        lax.fori_loop(1, NZ, one, 0)

    def y_rows(at):
        return pl.ds(LOCAL * at, LOCAL)

    def as_blocks(v):
        return v.reshape(BLOCKS, BROWS, LANES)

    def as_rows(v):
        return v.reshape(ROWS, LANES)

    def quarter(q):
        return pl.ds(LOCAL * q, LOCAL)

    def half(h):
        return pl.ds(HALF * h, HALF)

    to_z = (gz, zb, zs, zr_sem)

    def y_copy(j, d):
        to = lax.rem(y + d, NY)
        return push(
            yb.at[j, y_rows(to)], xb.at[tile(x, j, c), quarter(d)], ys.at[j, d], yr_sem.at[j, d],
            z * NY + to, tp,
        )

    def x_copy(j, q, way):
        if way == 0:
            src, to = xb.at[tile(x, j, c), quarter(q)], right_id
        elif way == 1:
            src, to = xb.at[tile(x, j, c), quarter(q)], left_id
        elif q % 2 == 0:
            src, to = xb.at[tile(left, j, c), quarter(q)], right_id
        else:
            src, to = xb.at[tile(right, j, c), quarter(q)], left_id
        return push(src, src, xs.at[j, way * NY + q], xr.at[j, way * NY + q], ep, to)

    def x_land(j, q, way):
        chip = (left, right, opp)[way]
        dst = xb.at[tile(chip, j, c), quarter(q)]
        return push(dst, dst, xs.at[j, way * NY + q], xr.at[j, way * NY + q], ep, tp)

    chips = {OPP: opp, RIGHT: right, LEFT: left, OWN: x}

    def c_copy(j, h, kind):
        src = xb.at[tile(chips[kind], j, c), half(h)]
        return push(src, src, cs.at[j, 4 * h + kind], cr.at[j, 4 * h + kind], ep, twin)

    def c_land(j, h, kind):
        dst = xb.at[tile(chips[kind], j, 1 - c), half(h)]
        return push(dst, dst, cs.at[j, 4 * h + kind], cr.at[j, 4 * h + kind], ep, tp)

    def gather(j):
        if j not in FIRST_OUT:
            fill(j)
        z_start(*to_z, j)

    to_z2 = (gz2, zb2, zs2, zr2)

    def y2_copy(j, d):
        to = lax.rem(y + d, NY)
        return push(
            yb2.at[j, y_rows(to)], xb.at[tile(opp, j, c), quarter(d)], ys2.at[j, d], yr2.at[j, d],
            z * NY + to, tp,
        )

    def gather2(j):
        tok2_copy(j).wait()
        rows = jnp.dot(place[...], tok2[j], preferred_element_type=F32)
        gz2[j] = as_blocks(rows.astype(BF16))
        z_start(*to_z2, j)

    def turn2(j):
        z_wait(*to_z2, j)
        rows = jnp.dot(perm[...], as_rows(zb2[j]), preferred_element_type=F32)
        yb2[j] = as_blocks(rows.astype(BF16))
        for d in (2, 1, 3):
            y2_copy(j, d).start()
        xb[tile(opp, j, c), quarter(0)] = yb2[j, y_rows(y)]

    def spread(j, q):
        x_copy(j, q, 0).start()
        x_copy(j, q, 1).start()

    def turn(j):
        z_wait(*to_z, j)
        rows = jnp.dot(perm[...], as_rows(zb[j]), preferred_element_type=F32)
        yb[j] = as_blocks(rows.astype(BF16))
        for d in (2, 1, 3):
            y_copy(j, d).start()
        xb[tile(x, j, c), quarter(0)] = yb[j, y_rows(y)]
        spread(j, 0)

    def side(j, q):
        y_copy(j, q).wait_recv()
        spread(j, q)
        if q < 3:
            c_copy(j, q // 2, OWN).start()

    def forward(j, q):
        x_land(j, q, q % 2).wait_recv()
        if j not in OVER_Z:
            x_copy(j, q, 2).start()

    def pass_left(j, h):
        x_land(j, 2 * h + 1, 0).wait_recv()
        c_copy(j, h, LEFT).start()

    def pass_right(j, h):
        x_land(j, 2 * h, 1).wait_recv()
        c_copy(j, h, RIGHT).start()

    def last_hop(j, h):
        if j in OVER_Z:
            for d in ((1,), (2, 3))[h]:
                y2_copy(j, d).wait_recv()
        else:
            x_land(j, 2 * h, 2).wait_recv()
            x_land(j, 2 * h + 1, 2).wait_recv()
        c_copy(j, h, OPP).start()

    def multiply(j, h):
        def landed():
            for kind in (OWN, LEFT, RIGHT, OPP):
                c_land(j, h, kind).wait_recv()

        if j < FIRST - 1:
            landed()
        else:
            pl.when(c == 1)(landed)
        tiles = [chip * TILES + j for chip in range(NX)]
        if j < FIRST - 1:
            tiles += [chip * TILES + FIRST + j for chip in range(NX)]
        for e in range(LOCAL):
            rows = jnp.concatenate(
                [
                    jnp.concatenate([xb[g, LOCAL * q + e] for q in (2 * h, 2 * h + 1)], axis=0)
                    for g in tiles
                ],
                axis=1,
            )
            weight = jnp.concatenate([up[e, g * LANES:(g + 1) * LANES, :] for g in tiles], axis=0)
            product = jnp.dot(rows, weight, preferred_element_type=F32)
            if j == FIRST_UP[h]:
                raised[h, e] = product
            elif j != LAST_UP[h]:
                raised[h, e] = raised[h, e] + product
            else:
                v = raised[h, e] + product
                hid[h, e] = (v / (1.0 + jnp.exp(-v))).astype(BF16)

    def make_perm():
        for b in range(BLOCKS):
            row = lax.broadcasted_iota(jnp.int32, (BROWS, 1), 0) + b * BROWS
            block = lax.shift_right_logical(row * 205, 11)
            source = (
                (lax.bitwise_and(block, 7) * BLOCKS + lax.shift_right_logical(block, 3)) * CAP
                + row - block * CAP
            )
            column = lax.broadcasted_iota(jnp.int32, (BROWS, ROWS), 1)
            perm[b * BROWS:(b + 1) * BROWS, :] = jnp.where(column == source, 1.0, 0.0).astype(BF16)

    def make_mix():
        rw_copy.wait()
        w0, w1 = rw_ref[0:1, :], rw_ref[1:2, :]
        for b in range(BLOCKS):
            at = lax.broadcasted_iota(jnp.int32, (BROWS, tokens), 0) + b * BROWS
            mix = jnp.where(at == pos0, w0, 0.0) + jnp.where(at == pos1, w1, 0.0)
            coarse = mix.astype(BF16)
            mixw[b * BROWS:(b + 1) * BROWS, 0:tokens] = coarse
            mixw[b * BROWS:(b + 1) * BROWS, tokens:] = (mix - coarse.astype(F32)).astype(BF16)

    back_z = (zo, zr, rzs, rzr)

    def rc_copy(j, h, kind):
        src = (other if j < FIRST - 1 else part).at[j, kind, half(h)]
        at = 4 * h + kind
        return push(src, cross.at[j, kind, half(h)], rcs.at[j, at], rcr.at[j, at], ep, twin)

    def rc_land(j, h, kind):
        dst = cross.at[j, kind, half(h)]
        at = 4 * h + kind
        return push(dst, dst, rcs.at[j, at], rcr.at[j, at], ep, tp)

    def rx_copy(j, h, kind):
        if kind == 0:
            src, dst, to = part.at[j, OPP, quarter(2 * h)], half_in.at[j, h, 0], right_id
        elif kind == 1:
            src, dst, to = part.at[j, OPP, quarter(2 * h + 1)], half_in.at[j, h, 1], left_id
        elif kind == 2:
            src, dst, to = part.at[j, RIGHT, half(h)], full_in.at[j, 0, half(h)], right_id
        else:
            src, dst, to = part.at[j, LEFT, half(h)], full_in.at[j, 1, half(h)], left_id
        at = 4 * h + kind
        return push(src, dst, rxs.at[j, at], rxr.at[j, at], ep, to)

    def ry_copy(j, d):
        to = lax.rem(y + NY - d, NY)
        return push(
            summed.at[j, quarter(d)], yr.at[j, y_rows(y)], rys.at[j, d], ryr.at[j, d],
            z * NY + to, tp,
        )

    def ry_land(j, d):
        dst = yr.at[j, y_rows(lax.rem(y + d, NY))]
        return push(dst, dst, rys.at[j, d], ryr.at[j, d], ep, tp)

    def lower(j, h, kind):
        chip = chips[kind]
        for e in range(LOCAL):
            mine = down[e, :, lanes(tile(chip, j, c if j < FIRST - 1 else 0))]
            if j < FIRST - 1:
                theirs = down[e, :, lanes(tile(chip, j, 1 - c))]
                weight = jnp.concatenate([mine, theirs], axis=1)
            else:
                weight = mine
            product = jnp.dot(hid[h, e], weight, preferred_element_type=F32).astype(BF16)
            for i in range(2):
                at = LOCAL * (2 * h + i) + e
                rows = product[i * BROWS:(i + 1) * BROWS]
                if j < FIRST - 1:
                    part[j, kind, at] = rows[:, :LANES]
                    other[j, kind, at] = rows[:, LANES:]
                else:
                    part[j, kind, at] = rows
        if j < FIRST - 1:
            rc_copy(j, h, kind).start()
        else:
            pl.when(c == 1)(lambda: rc_copy(j, h, kind).start())

    def wide(v):
        return v.astype(F32)

    def add_opp(j, h):
        rc_land(j, h, OPP).wait_recv()
        at = half(h)
        part[j, OPP, at] = (wide(part[j, OPP, at]) + wide(cross[j, OPP, at])).astype(BF16)
        rx_copy(j, h, 0).start()
        rx_copy(j, h, 1).start()

    def add_side(j, h, kind):
        way = 0 if kind == RIGHT else 1
        near, far = quarter(2 * h + way), quarter(2 * h + 1 - way)
        rc_land(j, h, kind).wait_recv()
        part[j, kind, far] = (wide(part[j, kind, far]) + wide(cross[j, kind, far])).astype(BF16)
        rx_copy(j, h, way).wait_recv()
        part[j, kind, near] = (
            wide(part[j, kind, near]) + wide(cross[j, kind, near]) + wide(half_in[j, h, way])
        ).astype(BF16)
        rx_copy(j, h, 2 + way).start()

    def add_own(j, h):
        rc_land(j, h, OWN).wait_recv()
        rx_copy(j, h, 2).wait_recv()
        rx_copy(j, h, 3).wait_recv()
        at = half(h)
        summed[j, at] = (
            (wide(part[j, OWN, at]) + wide(cross[j, OWN, at]))
            + (wide(full_in[j, 0, at]) + wide(full_in[j, 1, at]))
        ).astype(BF16)
        if h == 0:
            ry_copy(j, 1).start()
            yr[j, y_rows(y)] = summed[j, quarter(0)]
        else:
            ry_copy(j, 2).start()
            ry_copy(j, 3).start()

    def turn_back(j):
        for d in (1, 2, 3):
            ry_land(j, d).wait_recv()
        rows = jnp.dot(perm[...], as_rows(yr[j]), preferred_element_type=F32)
        zo[j] = as_blocks(rows.astype(BF16))
        z_start(*back_z, j)

    mid_copy = push(mid_out, mid_in, ms, mr, ep, twin)
    middle = LANES // 2

    def mix(j):
        z_wait(*back_z, j)
        both = lax.dot_general(
            as_rows(zr[j]), mixw[...], (((0,), (0,)), ((), ())), preferred_element_type=F32
        )
        result = (both[:, :tokens] + both[:, tokens:]).astype(BF16)
        if j == FIRST - 1:
            out_ref[j * LANES:j * LANES + middle, :] = result[:middle]
            mid_out[...] = result[middle:]
            mid_copy.start()
        else:
            def first():
                out_ref[j * LANES:(j + 1) * LANES, :] = result

            def second():
                out_ref[middle + j * LANES:middle + (j + 1) * LANES, :] = result

            pl.when(c == 0)(first)
            pl.when(c == 1)(second)

    def take_middle():
        mid_copy.wait_recv()
        out_ref[0:middle, :] = mid_in[...]

    def do(step, j, *h):
        owned(j, lambda: step(j, *h))

    do(gather, 2)
    make_perm()
    do(gather, 1)
    do(gather, 3)
    do(turn, 2)
    do(gather, 0)
    do(turn, 1)
    do(forward, 2, 0)
    do(side, 2, 1)
    do(side, 2, 3)
    do(gather2, 3)
    do(side, 2, 2)
    do(gather2, 0)
    do(turn, 3)
    do(side, 1, 1)
    do(side, 1, 3)
    do(forward, 2, 1)
    do(turn, 0)
    do(forward, 2, 2)
    do(side, 3, 1)
    do(turn2, 3)
    do(side, 3, 3)
    do(forward, 1, 0)
    do(forward, 2, 3)
    do(pass_right, 2, 0)
    do(pass_left, 2, 1)
    do(forward, 3, 0)
    do(pass_left, 2, 0)
    do(side, 1, 2)
    do(forward, 1, 1)
    do(forward, 0, 0)
    do(side, 0, 1)
    do(turn2, 0)
    do(pass_left, 3, 0)
    do(side, 0, 3)
    do(last_hop, 2, 0)
    do(pass_right, 2, 1)
    do(forward, 3, 3)
    do(side, 3, 2)
    do(forward, 3, 1)
    do(pass_right, 1, 0)
    do(last_hop, 2, 1)
    do(last_hop, 3, 0)
    do(pass_right, 3, 0)
    do(side, 0, 2)
    do(pass_left, 1, 0)
    up_copy.wait()
    multiply(2, 0)
    do(forward, 1, 3)
    do(forward, 1, 2)
    do(last_hop, 1, 0)
    multiply(2, 1)
    do(forward, 0, 1)
    do(pass_right, 1, 1)
    do(pass_right, 0, 0)
    do(pass_left, 0, 0)
    multiply(3, 0)
    do(last_hop, 0, 0)
    multiply(1, 0)
    do(forward, 3, 2)
    do(pass_left, 1, 1)
    do(pass_right, 3, 1)
    do(pass_left, 3, 1)
    do(last_hop, 3, 1)
    do(forward, 0, 3)
    do(forward, 0, 2)
    do(last_hop, 0, 1)
    do(pass_right, 0, 1)
    do(pass_left, 0, 1)
    multiply(0, 0)
    down_copy.wait()
    lower(0, 0, OPP)
    lower(2, 0, OPP)
    lower(1, 0, OPP)
    do(last_hop, 1, 1)
    multiply(3, 1)
    do(add_opp, 0, 0)
    multiply(0, 1)
    do(add_opp, 1, 0)
    multiply(1, 1)
    lower(0, 1, OPP)
    do(add_opp, 2, 0)
    lower(3, 1, RIGHT)
    lower(3, 1, OPP)
    lower(3, 0, OPP)
    lower(0, 0, LEFT)
    do(add_opp, 0, 1)
    lower(0, 0, RIGHT)
    lower(0, 0, OWN)
    do(add_opp, 3, 1)
    lower(1, 0, RIGHT)
    lower(0, 1, LEFT)
    do(add_opp, 3, 0)
    lower(0, 1, RIGHT)
    do(add_side, 0, 0, LEFT)
    lower(2, 1, OPP)
    do(add_side, 0, 0, RIGHT)
    lower(0, 1, OWN)
    lower(3, 1, LEFT)
    lower(1, 1, OPP)
    lower(2, 1, OWN)
    do(add_side, 0, 1, LEFT)
    do(add_side, 0, 1, RIGHT)
    lower(2, 1, LEFT)
    do(add_opp, 1, 1)
    do(add_opp, 2, 1)
    lower(2, 0, LEFT)
    lower(2, 1, RIGHT)
    lower(3, 0, LEFT)
    lower(1, 1, RIGHT)
    lower(2, 0, RIGHT)
    lower(3, 0, OWN)
    lower(1, 0, LEFT)
    lower(1, 1, LEFT)
    lower(3, 0, RIGHT)
    lower(3, 1, OWN)
    do(add_side, 3, 1, LEFT)
    lower(1, 0, OWN)
    do(add_side, 3, 1, RIGHT)
    lower(1, 1, OWN)
    do(add_side, 3, 0, LEFT)
    do(add_side, 3, 0, RIGHT)
    do(add_own, 0, 1)
    do(add_own, 0, 0)
    do(add_side, 1, 1, LEFT)
    do(add_side, 1, 0, LEFT)
    do(add_side, 1, 1, RIGHT)
    lower(2, 0, OWN)
    do(add_side, 1, 0, RIGHT)
    do(add_side, 2, 1, RIGHT)
    do(add_own, 3, 1)
    make_mix()
    do(add_side, 2, 0, RIGHT)
    do(add_own, 3, 0)
    do(add_side, 2, 1, LEFT)
    do(add_side, 2, 0, LEFT)
    do(turn_back, 0)
    do(turn_back, 3)
    do(add_own, 1, 1)
    do(add_own, 1, 0)
    do(add_own, 2, 1)
    do(add_own, 2, 0)
    do(turn_back, 1)
    do(mix, 3)
    do(mix, 0)
    do(turn_back, 2)
    pl.when(c == 1)(take_middle)
    do(mix, 1)
    do(mix, 2)

    def all_sent(j):
        z_sent(*to_z, j)
        z_sent(*back_z, j)
        if j in OVER_Z:
            z_sent(*to_z2, j)
        for d in range(1, NY):
            if j in OVER_Z:
                y2_copy(j, d).wait_send()
            y_copy(j, d).wait_send()
            ry_copy(j, d).wait_send()
        for q in range(NY):
            for way in range(2 if j in OVER_Z else 3):
                x_copy(j, q, way).wait_send()
        for h in range(2):
            for kind in range(4):
                c_copy(j, h, kind).wait_send()
                rx_copy(j, h, kind).wait_send()
                if j < FIRST - 1:
                    rc_copy(j, h, kind).wait_send()

    for j in range(FIRST):
        do(all_sent, j)
    pl.when(c == 0)(lambda: mid_copy.wait_send())

    def extras_sent():
        for h in range(2):
            for kind in range(4):
                rc_copy(FIRST - 1, h, kind).wait_send()

    pl.when(c == 1)(extras_sent)


def on_device(tokens, expert_ids, routing_weights, up_weight, down_weight):
    count, width = tokens.shape
    hidden = up_weight.shape[2]
    dma = pltpu.SemaphoreType.DMA
    blocks = (BLOCKS, BROWS, LANES)
    any_space = pl.BlockSpec(memory_space=pl.ANY)
    in_vmem = pl.BlockSpec(memory_space=pltpu.VMEM)
    per_z, per_y = dma((FIRST, NZ)), dma((FIRST, NY))
    by_way, by_kind = dma((FIRST, 3 * NY)), dma((FIRST, 8))
    tile_set = pltpu.VMEM((FIRST,) + blocks, BF16)
    kind_set = pltpu.VMEM((FIRST, 4) + blocks, BF16)
    return pl.pallas_call(
        kernel,
        out_shape=jax.ShapeDtypeStruct((width // (NX * NC), count), BF16),
        in_specs=[any_space] * 5,
        out_specs=in_vmem,
        scratch_shapes=[
            pltpu.VMEM((TOP, count), jnp.int32),
            pltpu.VMEM((TOP, count), F32),
            pltpu.VMEM((FIRST, count, LANES), BF16),
            pltpu.VMEM(up_weight.shape, BF16),
            pltpu.VMEM(down_weight.shape, BF16),
            pltpu.VMEM((ROWS, count), BF16),
            pltpu.VMEM((ROWS, ROWS), BF16),
            pltpu.VMEM((ROWS, 2 * count), BF16),
            pltpu.VMEM((FIRST, count, LANES), BF16),
            tile_set,
            tile_set,
            tile_set,
            tile_set,
            tile_set,
            tile_set,
            pltpu.VMEM((NX * TILES,) + blocks, BF16),
            pltpu.VMEM((2, LOCAL, ROWS // LOCAL // 2, hidden), F32),
            pltpu.VMEM((2, LOCAL, ROWS // LOCAL // 2, hidden), BF16),
            kind_set,
            pltpu.VMEM((FIRST - 1, 4) + blocks, BF16),
            kind_set,
            pltpu.VMEM((FIRST, 2, 2, LOCAL, BROWS, LANES), BF16),
            pltpu.VMEM((FIRST, 2) + blocks, BF16),
            tile_set,
            tile_set,
            tile_set,
            tile_set,
            pltpu.VMEM((LANES // 2, count), BF16),
            pltpu.VMEM((LANES // 2, count), BF16),
            dma((FIRST,)),
            dma((4,)),
            dma((FIRST,)), per_z, per_z, per_y, per_y,
            per_z, per_z, per_y, per_y, by_way, by_way, by_kind, by_kind,
            by_kind, by_kind, by_kind, by_kind, per_y, per_y, per_z, per_z, dma, dma,
        ],
        compiler_params=pltpu.CompilerParams(
            collective_id=0, has_side_effects=True, vmem_limit_bytes=52 * 1024 * 1024
        ),
        cost_estimate=pl.CostEstimate(
            flops=4 * ROWS * width * hidden, bytes_accessed=8 * width * hidden, transcendentals=0
        ),
        name="experts",
    )(expert_ids.T, routing_weights.T, tokens, up_weight, down_weight).T


def solution(mesh):
    placed = (P("ep", None), P("ep", None), P("ep", None), P("ep", None, "tp"), P("ep", "tp", None))
    return jax.shard_map(
        on_device, mesh=mesh, in_specs=placed, out_specs=P("ep", "tp"), check_vma=False
    )
```

```python
import jax
import jax.numpy as jnp
from jax import lax
from jax.experimental import pallas as pl
from jax.experimental.pallas import tpu as pltpu
from jax.sharding import PartitionSpec as P

MESH = pl.DeviceIdType.MESH
BF16 = jnp.bfloat16
F32 = jnp.float32

NZ, NY, NX, NC = 8, 4, 4, 2
TOP = 2
LOCAL = 2
CAP = 10
LANES = 128
TILES = 7
FIRST = 4
BLOCKS = 8
BROWS = 80
ROWS = BLOCKS * BROWS
HALF = BLOCKS // 2
OPP, RIGHT, LEFT, OWN = 0, 1, 2, 3
LATE = (0, 2)
FIRST_OUT = (2, 1)
OVER_Z = (0, 3,)
FIRST_UP, LAST_UP = (2, 2), (0, 0)


def kernel(
    ids_hbm, rw_hbm, tok_hbm, up_hbm, down_hbm, out_ref,
    ids_ref, rw_ref, tok, up, down, place, perm, mixw,
    tok2, gz2, zb2, yb2, gz, zb, yb, xb, raised, hid,
    part, other, cross, half_in, full_in, summed, yr, zo, zr, mid_in, mid_out,
    tok_sem, w_sem,
    tok2_sem, zs2, zr2, ys2, yr2,
    zs, zr_sem, ys, yr_sem, xs, xr, cs, cr,
    rcs, rcr, rxs, rxr, rys, ryr, rzs, rzr, ms, mr,
):
    ep = lax.axis_index("ep")
    tp = lax.axis_index("tp")
    z, y = lax.div(ep, NY), lax.rem(ep, NY)
    x, c = lax.div(tp, NC), lax.rem(tp, NC)
    right, left, opp = lax.rem(x + 1, NX), lax.rem(x + 3, NX), lax.rem(x + 2, NX)
    twin = x * NC + (1 - c)
    right_id, left_id = right * NC + c, left * NC + c

    def tile(chip, j, core):
        return chip * TILES + core * FIRST + j

    def lanes(g):
        return pl.ds(pl.multiple_of(g * LANES, LANES), LANES)

    def push(src, dst, send, recv, to_ep, to_tp):
        return pltpu.make_async_remote_copy(
            src_ref=src, dst_ref=dst, send_sem=send, recv_sem=recv,
            device_id=(to_ep, to_tp), device_id_type=MESH,
        )

    def owned(j, body):
        if j < FIRST - 1:
            body()
        else:
            pl.when(c == 0)(body)

    barrier = pltpu.get_barrier_semaphore()

    def greet(to_ep, to_tp):
        pl.semaphore_signal(barrier, inc=1, device_id=(to_ep, to_tp), device_id_type=MESH)

    def greet_z(d, _):
        greet(lax.rem(z + d, NZ) * NY + y, tp)
        return 0

    def greet_y(d, _):
        greet(z * NY + lax.rem(y + d, NY), tp)
        return 0

    lax.fori_loop(1, NZ, greet_z, 0)
    lax.fori_loop(1, NY, greet_y, 0)
    greet(ep, right_id)
    greet(ep, left_id)
    greet(ep, twin)

    ids_copy = pltpu.make_async_copy(ids_hbm, ids_ref, w_sem.at[2])
    rw_copy = pltpu.make_async_copy(rw_hbm, rw_ref, w_sem.at[3])
    ids_copy.start()
    rw_copy.start()

    def tok_copy(j):
        return pltpu.make_async_copy(tok_hbm.at[:, lanes(tile(x, j, c))], tok.at[j], tok_sem.at[j])

    def tok2_copy(j):
        return pltpu.make_async_copy(
            tok_hbm.at[:, lanes(tile(opp, j, c))], tok2.at[j], tok2_sem.at[j]
        )

    for j in FIRST_OUT + tuple(j for j in range(FIRST) if j not in FIRST_OUT):
        owned(j, lambda j=j: tok_copy(j).start())
    for j in OVER_Z:
        owned(j, lambda j=j: tok2_copy(j).start())
    up_copy = pltpu.make_async_copy(up_hbm, up, w_sem.at[0])
    down_copy = pltpu.make_async_copy(down_hbm, down, w_sem.at[1])
    up_copy.start()
    down_copy.start()

    tokens = ids_ref.shape[1]
    experts = LOCAL * NZ * NY
    ids_copy.wait()
    ids0, ids1 = ids_ref[0:1, :], ids_ref[1:2, :]
    named = lax.broadcasted_iota(jnp.int32, (experts, tokens), 0)
    hot0 = (named == ids0).astype(F32)
    hot1 = (named == ids1).astype(F32)
    before = (
        lax.broadcasted_iota(jnp.int32, (tokens, tokens), 0)
        < lax.broadcasted_iota(jnp.int32, (tokens, tokens), 1)
    ).astype(F32).astype(BF16)
    earlier = jnp.dot((hot0 + hot1).astype(BF16), before, preferred_element_type=F32)
    within0 = jnp.sum(hot0 * earlier, axis=0, keepdims=True).astype(jnp.int32)
    within1 = jnp.sum(hot1 * earlier, axis=0, keepdims=True).astype(jnp.int32)
    pos0 = ids0 * CAP + within0
    pos1 = ids1 * CAP + within1
    for b in range(BLOCKS):
        at = lax.broadcasted_iota(jnp.int32, (BROWS, tokens), 0) + b * BROWS
        hits = jnp.where(at == pos0, 1.0, 0.0) + jnp.where(at == pos1, 1.0, 0.0)
        place[b * BROWS:(b + 1) * BROWS, :] = hits.astype(BF16)

    def fill(j):
        tok_copy(j).wait()
        rows = jnp.dot(place[...], tok[j], preferred_element_type=F32)
        gz[j] = rows.astype(BF16).reshape(BLOCKS, BROWS, LANES)

    for j in FIRST_OUT:
        owned(j, lambda j=j: fill(j))

    pl.semaphore_wait(barrier, (NZ - 1) + (NY - 1) + 3)

    def z_copy(src, dst, send, recv, j, d):
        to = lax.rem(z + d, NZ)
        return push(src.at[j, to], dst.at[j, z], send.at[j, d], recv.at[j, d], to * NY + y, tp)

    def z_land(src, dst, send, recv, j, d):
        of = lax.rem(z + NZ - d, NZ)
        return push(src.at[j, of], dst.at[j, of], send.at[j, d], recv.at[j, d], ep, tp)

    def z_start(src, dst, send, recv, j):
        def one(d, _):
            z_copy(src, dst, send, recv, j, d).start()
            return 0

        lax.fori_loop(1, NZ, one, 0)
        dst[j, z] = src[j, z]

    def z_wait(src, dst, send, recv, j):
        def one(d, _):
            z_land(src, dst, send, recv, j, d).wait_recv()
            return 0

        lax.fori_loop(1, NZ, one, 0)

    def z_sent(src, dst, send, recv, j):
        def one(d, _):
            z_copy(src, dst, send, recv, j, d).wait_send()
            return 0

        lax.fori_loop(1, NZ, one, 0)

    def y_rows(at):
        return pl.ds(LOCAL * at, LOCAL)

    def as_blocks(v):
        return v.reshape(BLOCKS, BROWS, LANES)

    def as_rows(v):
        return v.reshape(ROWS, LANES)

    def quarter(q):
        return pl.ds(LOCAL * q, LOCAL)

    def half(h):
        return pl.ds(HALF * h, HALF)

    to_z = (gz, zb, zs, zr_sem)

    def y_copy(j, d):
        to = lax.rem(y + d, NY)
        return push(
            yb.at[j, y_rows(to)], xb.at[tile(x, j, c), quarter(d)], ys.at[j, d], yr_sem.at[j, d],
            z * NY + to, tp,
        )

    def x_copy(j, q, way):
        if way == 0:
            src, to = xb.at[tile(x, j, c), quarter(q)], right_id
        elif way == 1:
            src, to = xb.at[tile(x, j, c), quarter(q)], left_id
        elif q % 2 == 0:
            src, to = xb.at[tile(left, j, c), quarter(q)], right_id
        else:
            src, to = xb.at[tile(right, j, c), quarter(q)], left_id
        return push(src, src, xs.at[j, way * NY + q], xr.at[j, way * NY + q], ep, to)

    def x_land(j, q, way):
        chip = (left, right, opp)[way]
        dst = xb.at[tile(chip, j, c), quarter(q)]
        return push(dst, dst, xs.at[j, way * NY + q], xr.at[j, way * NY + q], ep, tp)

    chips = {OPP: opp, RIGHT: right, LEFT: left, OWN: x}

    def c_copy(j, h, kind):
        src = xb.at[tile(chips[kind], j, c), half(h)]
        return push(src, src, cs.at[j, 4 * h + kind], cr.at[j, 4 * h + kind], ep, twin)

    def c_land(j, h, kind):
        dst = xb.at[tile(chips[kind], j, 1 - c), half(h)]
        return push(dst, dst, cs.at[j, 4 * h + kind], cr.at[j, 4 * h + kind], ep, tp)

    def gather(j):
        if j not in FIRST_OUT:
            fill(j)
        z_start(*to_z, j)

    to_z2 = (gz2, zb2, zs2, zr2)

    def y2_copy(j, d):
        to = lax.rem(y + d, NY)
        return push(
            yb2.at[j, y_rows(to)], xb.at[tile(opp, j, c), quarter(d)], ys2.at[j, d], yr2.at[j, d],
            z * NY + to, tp,
        )

    def gather2(j):
        tok2_copy(j).wait()
        rows = jnp.dot(place[...], tok2[j], preferred_element_type=F32)
        gz2[j] = as_blocks(rows.astype(BF16))
        z_start(*to_z2, j)

    def turn2(j):
        z_wait(*to_z2, j)
        rows = jnp.dot(perm[...], as_rows(zb2[j]), preferred_element_type=F32)
        yb2[j] = as_blocks(rows.astype(BF16))
        for d in (2, 1, 3):
            y2_copy(j, d).start()
        xb[tile(opp, j, c), quarter(0)] = yb2[j, y_rows(y)]

    def spread(j, q):
        x_copy(j, q, 0).start()
        x_copy(j, q, 1).start()

    def turn(j):
        z_wait(*to_z, j)
        rows = jnp.dot(perm[...], as_rows(zb[j]), preferred_element_type=F32)
        yb[j] = as_blocks(rows.astype(BF16))
        for d in (2, 1, 3):
            y_copy(j, d).start()
        xb[tile(x, j, c), quarter(0)] = yb[j, y_rows(y)]
        spread(j, 0)

    def side(j, q):
        y_copy(j, q).wait_recv()
        spread(j, q)
        if q < 3:
            c_copy(j, q // 2, OWN).start()

    def forward(j, q):
        x_land(j, q, q % 2).wait_recv()
        if j not in OVER_Z:
            x_copy(j, q, 2).start()

    def pass_left(j, h):
        x_land(j, 2 * h + 1, 0).wait_recv()
        c_copy(j, h, LEFT).start()

    def pass_right(j, h):
        x_land(j, 2 * h, 1).wait_recv()
        c_copy(j, h, RIGHT).start()

    def last_hop(j, h):
        if j in OVER_Z:
            for d in ((1,), (2, 3))[h]:
                y2_copy(j, d).wait_recv()
        else:
            x_land(j, 2 * h, 2).wait_recv()
            x_land(j, 2 * h + 1, 2).wait_recv()
        c_copy(j, h, OPP).start()

    def multiply(j, h):
        def landed():
            for kind in (OWN, LEFT, RIGHT, OPP):
                c_land(j, h, kind).wait_recv()

        if j < FIRST - 1:
            landed()
        else:
            pl.when(c == 1)(landed)
        tiles = [chip * TILES + j for chip in range(NX)]
        if j < FIRST - 1:
            tiles += [chip * TILES + FIRST + j for chip in range(NX)]
        for e in range(LOCAL):
            rows = jnp.concatenate(
                [
                    jnp.concatenate([xb[g, LOCAL * q + e] for q in (2 * h, 2 * h + 1)], axis=0)
                    for g in tiles
                ],
                axis=1,
            )
            weight = jnp.concatenate([up[e, g * LANES:(g + 1) * LANES, :] for g in tiles], axis=0)
            product = jnp.dot(rows, weight, preferred_element_type=F32)
            if j == FIRST_UP[h]:
                raised[h, e] = product
            elif j != LAST_UP[h]:
                raised[h, e] = raised[h, e] + product
            else:
                v = raised[h, e] + product
                hid[h, e] = (v / (1.0 + jnp.exp(-v))).astype(BF16)

    def make_perm():
        for b in range(BLOCKS):
            row = lax.broadcasted_iota(jnp.int32, (BROWS, 1), 0) + b * BROWS
            block = lax.shift_right_logical(row * 205, 11)
            source = (
                (lax.bitwise_and(block, 7) * BLOCKS + lax.shift_right_logical(block, 3)) * CAP
                + row - block * CAP
            )
            column = lax.broadcasted_iota(jnp.int32, (BROWS, ROWS), 1)
            perm[b * BROWS:(b + 1) * BROWS, :] = jnp.where(column == source, 1.0, 0.0).astype(BF16)

    def make_mix():
        rw_copy.wait()
        w0, w1 = rw_ref[0:1, :], rw_ref[1:2, :]
        for b in range(BLOCKS):
            at = lax.broadcasted_iota(jnp.int32, (BROWS, tokens), 0) + b * BROWS
            mix = jnp.where(at == pos0, w0, 0.0) + jnp.where(at == pos1, w1, 0.0)
            coarse = mix.astype(BF16)
            mixw[b * BROWS:(b + 1) * BROWS, 0:tokens] = coarse
            mixw[b * BROWS:(b + 1) * BROWS, tokens:] = (mix - coarse.astype(F32)).astype(BF16)

    back_z = (zo, zr, rzs, rzr)

    def rc_copy(j, h, kind):
        src = (other if j < FIRST - 1 else part).at[j, kind, half(h)]
        at = 4 * h + kind
        return push(src, cross.at[j, kind, half(h)], rcs.at[j, at], rcr.at[j, at], ep, twin)

    def rc_land(j, h, kind):
        dst = cross.at[j, kind, half(h)]
        at = 4 * h + kind
        return push(dst, dst, rcs.at[j, at], rcr.at[j, at], ep, tp)

    def rx_copy(j, h, kind):
        if kind == 0:
            src, dst, to = part.at[j, OPP, quarter(2 * h)], half_in.at[j, h, 0], right_id
        elif kind == 1:
            src, dst, to = part.at[j, OPP, quarter(2 * h + 1)], half_in.at[j, h, 1], left_id
        elif kind == 2:
            src, dst, to = part.at[j, RIGHT, half(h)], full_in.at[j, 0, half(h)], right_id
        else:
            src, dst, to = part.at[j, LEFT, half(h)], full_in.at[j, 1, half(h)], left_id
        at = 4 * h + kind
        return push(src, dst, rxs.at[j, at], rxr.at[j, at], ep, to)

    def ry_copy(j, d):
        to = lax.rem(y + NY - d, NY)
        return push(
            summed.at[j, quarter(d)], yr.at[j, y_rows(y)], rys.at[j, d], ryr.at[j, d],
            z * NY + to, tp,
        )

    def ry_land(j, d):
        dst = yr.at[j, y_rows(lax.rem(y + d, NY))]
        return push(dst, dst, rys.at[j, d], ryr.at[j, d], ep, tp)

    def lower(j, h, kind):
        chip = chips[kind]
        for e in range(LOCAL):
            mine = down[e, :, lanes(tile(chip, j, c if j < FIRST - 1 else 0))]
            if j < FIRST - 1:
                theirs = down[e, :, lanes(tile(chip, j, 1 - c))]
                weight = jnp.concatenate([mine, theirs], axis=1)
            else:
                weight = mine
            product = jnp.dot(hid[h, e], weight, preferred_element_type=F32).astype(BF16)
            for i in range(2):
                at = LOCAL * (2 * h + i) + e
                rows = product[i * BROWS:(i + 1) * BROWS]
                if j < FIRST - 1:
                    part[j, kind, at] = rows[:, :LANES]
                    other[j, kind, at] = rows[:, LANES:]
                else:
                    part[j, kind, at] = rows
        if j < FIRST - 1:
            rc_copy(j, h, kind).start()
        else:
            pl.when(c == 1)(lambda: rc_copy(j, h, kind).start())

    def wide(v):
        return v.astype(F32)

    def add_opp(j, h):
        rc_land(j, h, OPP).wait_recv()
        at = half(h)
        part[j, OPP, at] = (wide(part[j, OPP, at]) + wide(cross[j, OPP, at])).astype(BF16)
        rx_copy(j, h, 0).start()
        rx_copy(j, h, 1).start()

    def add_side(j, h, kind):
        way = 0 if kind == RIGHT else 1
        near, far = quarter(2 * h + way), quarter(2 * h + 1 - way)
        rc_land(j, h, kind).wait_recv()
        part[j, kind, far] = (wide(part[j, kind, far]) + wide(cross[j, kind, far])).astype(BF16)
        rx_copy(j, h, way).wait_recv()
        part[j, kind, near] = (
            wide(part[j, kind, near]) + wide(cross[j, kind, near]) + wide(half_in[j, h, way])
        ).astype(BF16)
        rx_copy(j, h, 2 + way).start()

    def add_own(j, h):
        rc_land(j, h, OWN).wait_recv()
        rx_copy(j, h, 2).wait_recv()
        rx_copy(j, h, 3).wait_recv()
        at = half(h)
        summed[j, at] = (
            (wide(part[j, OWN, at]) + wide(cross[j, OWN, at]))
            + (wide(full_in[j, 0, at]) + wide(full_in[j, 1, at]))
        ).astype(BF16)
        if h == 0:
            ry_copy(j, 1).start()
            yr[j, y_rows(y)] = summed[j, quarter(0)]
        else:
            ry_copy(j, 2).start()
            ry_copy(j, 3).start()

    def turn_back(j):
        for d in (1, 2, 3):
            ry_land(j, d).wait_recv()
        rows = jnp.dot(perm[...], as_rows(yr[j]), preferred_element_type=F32)
        zo[j] = as_blocks(rows.astype(BF16))
        z_start(*back_z, j)

    mid_copy = push(mid_out, mid_in, ms, mr, ep, twin)
    middle = LANES // 2

    def mix(j):
        z_wait(*back_z, j)
        both = lax.dot_general(
            as_rows(zr[j]), mixw[...], (((0,), (0,)), ((), ())), preferred_element_type=F32
        )
        result = (both[:, :tokens] + both[:, tokens:]).astype(BF16)
        if j == FIRST - 1:
            out_ref[j * LANES:j * LANES + middle, :] = result[:middle]
            mid_out[...] = result[middle:]
            mid_copy.start()
        else:
            def first():
                out_ref[j * LANES:(j + 1) * LANES, :] = result

            def second():
                out_ref[middle + j * LANES:middle + (j + 1) * LANES, :] = result

            pl.when(c == 0)(first)
            pl.when(c == 1)(second)

    def take_middle():
        mid_copy.wait_recv()
        out_ref[0:middle, :] = mid_in[...]

    def do(step, j, *h):
        owned(j, lambda: step(j, *h))

    def all_sent(j):
        z_sent(*to_z, j)
        if j not in LATE:
            z_sent(*back_z, j)
        if j in OVER_Z:
            z_sent(*to_z2, j)
        for d in range(1, NY):
            if j in OVER_Z:
                y2_copy(j, d).wait_send()
            y_copy(j, d).wait_send()
            ry_copy(j, d).wait_send()
        for q in range(NY):
            for way in range(2 if j in OVER_Z else 3):
                x_copy(j, q, way).wait_send()
        for h in range(2):
            for kind in range(4):
                c_copy(j, h, kind).wait_send()
                rx_copy(j, h, kind).wait_send()
                if j < FIRST - 1:
                    rc_copy(j, h, kind).wait_send()

    def extras_sent():
        for h in range(2):
            for kind in range(4):
                rc_copy(FIRST - 1, h, kind).wait_send()


    do(gather, 2)
    do(gather, 1)
    do(gather, 3)
    make_perm()
    do(turn, 2)
    do(gather, 0)
    do(turn, 1)
    do(side, 2, 1)
    do(side, 2, 3)
    do(forward, 2, 0)
    do(side, 2, 2)
    do(gather2, 3)
    do(gather2, 0)
    do(turn, 3)
    do(side, 1, 3)
    do(forward, 2, 1)
    do(side, 1, 1)
    do(pass_left, 2, 0)
    do(turn, 0)
    do(side, 3, 1)
    do(forward, 2, 3)
    do(forward, 2, 2)
    do(pass_right, 2, 0)
    do(side, 1, 2)
    do(turn2, 3)
    do(forward, 3, 0)
    do(side, 0, 1)
    do(side, 3, 3)
    do(forward, 1, 1)
    do(side, 3, 2)
    do(pass_left, 2, 1)
    do(forward, 1, 0)
    do(turn2, 0)
    do(forward, 3, 1)
    do(pass_right, 2, 1)
    do(last_hop, 2, 0)
    do(forward, 1, 3)
    do(side, 0, 3)
    do(forward, 1, 2)
    do(last_hop, 2, 1)
    do(last_hop, 3, 0)
    do(pass_right, 1, 0)
    do(pass_right, 1, 1)
    do(pass_right, 3, 0)
    do(side, 0, 2)
    do(forward, 0, 0)
    do(pass_left, 3, 0)
    do(pass_left, 1, 1)
    do(pass_left, 1, 0)
    up_copy.wait()
    multiply(2, 0)
    do(forward, 0, 1)
    do(pass_left, 0, 0)
    do(last_hop, 1, 0)
    do(forward, 3, 3)
    do(forward, 3, 2)
    do(pass_right, 3, 1)
    do(pass_right, 0, 0)
    multiply(2, 1)
    do(pass_left, 3, 1)
    do(last_hop, 0, 0)
    do(last_hop, 3, 1)
    multiply(3, 0)
    multiply(1, 0)
    do(last_hop, 1, 1)
    multiply(0, 0)
    down_copy.wait()
    lower(1, 0, OPP)
    do(forward, 0, 3)
    lower(2, 0, OPP)
    do(forward, 0, 2)
    do(last_hop, 0, 1)
    do(pass_right, 0, 1)
    do(pass_left, 0, 1)
    multiply(3, 1)
    lower(0, 0, OPP)
    do(add_opp, 1, 0)
    multiply(1, 1)
    do(add_opp, 2, 0)
    multiply(0, 1)
    lower(1, 1, OPP)
    lower(3, 1, OPP)
    do(add_opp, 0, 0)
    lower(3, 1, OWN)
    lower(2, 1, RIGHT)
    lower(1, 0, RIGHT)
    lower(3, 1, RIGHT)
    lower(1, 0, LEFT)
    do(add_opp, 3, 1)
    do(add_opp, 1, 1)
    lower(3, 0, OPP)
    lower(1, 1, RIGHT)
    lower(2, 1, OWN)
    lower(1, 1, LEFT)
    lower(2, 0, LEFT)
    do(add_side, 1, 0, RIGHT)
    lower(0, 0, RIGHT)
    lower(0, 1, OPP)
    do(add_opp, 3, 0)
    do(add_side, 1, 0, LEFT)
    lower(2, 1, LEFT)
    lower(3, 0, LEFT)
    lower(0, 1, RIGHT)
    lower(1, 0, OWN)
    lower(2, 1, OPP)
    make_mix()
    lower(0, 1, LEFT)
    do(add_side, 1, 1, LEFT)
    do(add_side, 1, 1, RIGHT)
    lower(3, 1, LEFT)
    do(add_opp, 0, 1)
    do(add_side, 3, 1, LEFT)
    lower(0, 0, OWN)
    do(add_opp, 2, 1)
    lower(1, 1, OWN)
    do(add_side, 3, 0, LEFT)
    do(add_side, 3, 1, RIGHT)
    lower(3, 0, RIGHT)
    do(add_own, 1, 0)
    lower(0, 0, LEFT)
    lower(2, 0, RIGHT)
    lower(0, 1, OWN)
    do(add_side, 3, 0, RIGHT)
    do(add_own, 1, 1)
    do(add_side, 0, 1, LEFT)
    do(add_side, 0, 1, RIGHT)
    lower(2, 0, OWN)
    do(add_side, 0, 0, LEFT)
    do(add_side, 0, 0, RIGHT)
    lower(3, 0, OWN)
    do(add_side, 2, 1, RIGHT)
    do(add_own, 3, 1)
    do(add_side, 2, 1, LEFT)
    do(add_side, 2, 0, LEFT)
    do(add_own, 3, 0)
    do(add_side, 2, 0, RIGHT)
    do(turn_back, 1)
    do(turn_back, 3)
    do(add_own, 0, 1)
    do(add_own, 0, 0)
    do(add_own, 2, 1)
    do(add_own, 2, 0)
    do(turn_back, 0)
    do(mix, 3)
    do(turn_back, 2)
    pl.when(c == 1)(take_middle)
    do(mix, 1)
    do(mix, 0)
    for j in range(FIRST):
        do(all_sent, j)
    pl.when(c == 1)(extras_sent)
    do(mix, 2)

    for j in LATE:
        do(lambda j: z_sent(*back_z, j), j)
    pl.when(c == 0)(lambda: mid_copy.wait_send())


def on_device(tokens, expert_ids, routing_weights, up_weight, down_weight):
    count, width = tokens.shape
    hidden = up_weight.shape[2]
    dma = pltpu.SemaphoreType.DMA
    blocks = (BLOCKS, BROWS, LANES)
    any_space = pl.BlockSpec(memory_space=pl.ANY)
    in_vmem = pl.BlockSpec(memory_space=pltpu.VMEM)
    per_z, per_y = dma((FIRST, NZ)), dma((FIRST, NY))
    by_way, by_kind = dma((FIRST, 3 * NY)), dma((FIRST, 8))
    tile_set = pltpu.VMEM((FIRST,) + blocks, BF16)
    kind_set = pltpu.VMEM((FIRST, 4) + blocks, BF16)
    return pl.pallas_call(
        kernel,
        out_shape=jax.ShapeDtypeStruct((width // (NX * NC), count), BF16),
        in_specs=[any_space] * 5,
        out_specs=in_vmem,
        scratch_shapes=[
            pltpu.VMEM((TOP, count), jnp.int32),
            pltpu.VMEM((TOP, count), F32),
            pltpu.VMEM((FIRST, count, LANES), BF16),
            pltpu.VMEM(up_weight.shape, BF16),
            pltpu.VMEM(down_weight.shape, BF16),
            pltpu.VMEM((ROWS, count), BF16),
            pltpu.VMEM((ROWS, ROWS), BF16),
            pltpu.VMEM((ROWS, 2 * count), BF16),
            pltpu.VMEM((FIRST, count, LANES), BF16),
            tile_set,
            tile_set,
            tile_set,
            tile_set,
            tile_set,
            tile_set,
            pltpu.VMEM((NX * TILES,) + blocks, BF16),
            pltpu.VMEM((2, LOCAL, ROWS // LOCAL // 2, hidden), F32),
            pltpu.VMEM((2, LOCAL, ROWS // LOCAL // 2, hidden), BF16),
            kind_set,
            pltpu.VMEM((FIRST - 1, 4) + blocks, BF16),
            kind_set,
            pltpu.VMEM((FIRST, 2, 2, LOCAL, BROWS, LANES), BF16),
            pltpu.VMEM((FIRST, 2) + blocks, BF16),
            tile_set,
            tile_set,
            tile_set,
            tile_set,
            pltpu.VMEM((LANES // 2, count), BF16),
            pltpu.VMEM((LANES // 2, count), BF16),
            dma((FIRST,)),
            dma((4,)),
            dma((FIRST,)), per_z, per_z, per_y, per_y,
            per_z, per_z, per_y, per_y, by_way, by_way, by_kind, by_kind,
            by_kind, by_kind, by_kind, by_kind, per_y, per_y, per_z, per_z, dma, dma,
        ],
        compiler_params=pltpu.CompilerParams(
            collective_id=0, has_side_effects=True, vmem_limit_bytes=52 * 1024 * 1024
        ),
        cost_estimate=pl.CostEstimate(
            flops=4 * ROWS * width * hidden, bytes_accessed=8 * width * hidden, transcendentals=0
        ),
        name="experts",
    )(expert_ids.T, routing_weights.T, tokens, up_weight, down_weight).T


def solution(mesh):
    placed = (P("ep", None), P("ep", None), P("ep", None), P("ep", None, "tp"), P("ep", "tp", None))
    return jax.shard_map(
        on_device, mesh=mesh, in_specs=placed, out_specs=P("ep", "tp"), check_vma=False
    )
```

```python
import jax
import jax.numpy as jnp
from jax import lax
from jax.experimental import pallas as pl
from jax.experimental.pallas import tpu as pltpu
from jax.sharding import PartitionSpec as P

MESH = pl.DeviceIdType.MESH
BF16 = jnp.bfloat16
F32 = jnp.float32

NZ, NY, NX, NC = 8, 4, 4, 2
TOP = 2
LOCAL = 2
CAP = 10
LANES = 128
TILES = 7
FIRST = 4
BLOCKS = 8
BROWS = 80
ROWS = BLOCKS * BROWS
HALF = BLOCKS // 2
OPP, RIGHT, LEFT, OWN = 0, 1, 2, 3
LATE = (1, 2)
FIRST_OUT = (2, 1)
OVER_Z = (0, 3,)
FIRST_UP, LAST_UP = (2, 2), (0, 1)


def kernel(
    ids_hbm, rw_hbm, tok_hbm, up_hbm, down_hbm, out_ref,
    ids_ref, rw_ref, tok, up, down, place, perm, mixw,
    tok2, gz2, zb2, yb2, gz, zb, yb, xb, raised, hid,
    part, other, cross, half_in, full_in, summed, yr, zo, zr, mid_in, mid_out,
    tok_sem, w_sem,
    tok2_sem, zs2, zr2, ys2, yr2,
    zs, zr_sem, ys, yr_sem, xs, xr, cs, cr,
    rcs, rcr, rxs, rxr, rys, ryr, rzs, rzr, ms, mr,
):
    ep = lax.axis_index("ep")
    tp = lax.axis_index("tp")
    z, y = lax.div(ep, NY), lax.rem(ep, NY)
    x, c = lax.div(tp, NC), lax.rem(tp, NC)
    right, left, opp = lax.rem(x + 1, NX), lax.rem(x + 3, NX), lax.rem(x + 2, NX)
    twin = x * NC + (1 - c)
    right_id, left_id = right * NC + c, left * NC + c

    def tile(chip, j, core):
        return chip * TILES + core * FIRST + j

    def lanes(g):
        return pl.ds(pl.multiple_of(g * LANES, LANES), LANES)

    def push(src, dst, send, recv, to_ep, to_tp):
        return pltpu.make_async_remote_copy(
            src_ref=src, dst_ref=dst, send_sem=send, recv_sem=recv,
            device_id=(to_ep, to_tp), device_id_type=MESH,
        )

    def owned(j, body):
        if j < FIRST - 1:
            body()
        else:
            pl.when(c == 0)(body)

    barrier = pltpu.get_barrier_semaphore()

    def greet(to_ep, to_tp):
        pl.semaphore_signal(barrier, inc=1, device_id=(to_ep, to_tp), device_id_type=MESH)

    def greet_z(d, _):
        greet(lax.rem(z + d, NZ) * NY + y, tp)
        return 0

    def greet_y(d, _):
        greet(z * NY + lax.rem(y + d, NY), tp)
        return 0

    lax.fori_loop(1, NZ, greet_z, 0)
    lax.fori_loop(1, NY, greet_y, 0)
    greet(ep, right_id)
    greet(ep, left_id)
    greet(ep, twin)

    ids_copy = pltpu.make_async_copy(ids_hbm, ids_ref, w_sem.at[2])
    rw_copy = pltpu.make_async_copy(rw_hbm, rw_ref, w_sem.at[3])
    ids_copy.start()
    rw_copy.start()

    def tok_copy(j):
        return pltpu.make_async_copy(tok_hbm.at[:, lanes(tile(x, j, c))], tok.at[j], tok_sem.at[j])

    def tok2_copy(j):
        return pltpu.make_async_copy(
            tok_hbm.at[:, lanes(tile(opp, j, c))], tok2.at[j], tok2_sem.at[j]
        )

    for j in FIRST_OUT + tuple(j for j in range(FIRST) if j not in FIRST_OUT):
        owned(j, lambda j=j: tok_copy(j).start())
    for j in OVER_Z:
        owned(j, lambda j=j: tok2_copy(j).start())
    up_copy = pltpu.make_async_copy(up_hbm, up, w_sem.at[0])
    down_copy = pltpu.make_async_copy(down_hbm, down, w_sem.at[1])
    up_copy.start()
    down_copy.start()

    tokens = ids_ref.shape[1]
    experts = LOCAL * NZ * NY
    ids_copy.wait()
    ids0, ids1 = ids_ref[0:1, :], ids_ref[1:2, :]
    named = lax.broadcasted_iota(jnp.int32, (experts, tokens), 0)
    hot0 = (named == ids0).astype(F32)
    hot1 = (named == ids1).astype(F32)
    before = (
        lax.broadcasted_iota(jnp.int32, (tokens, tokens), 0)
        < lax.broadcasted_iota(jnp.int32, (tokens, tokens), 1)
    ).astype(F32).astype(BF16)
    earlier = jnp.dot((hot0 + hot1).astype(BF16), before, preferred_element_type=F32)
    within0 = jnp.sum(hot0 * earlier, axis=0, keepdims=True).astype(jnp.int32)
    within1 = jnp.sum(hot1 * earlier, axis=0, keepdims=True).astype(jnp.int32)
    pos0 = ids0 * CAP + within0
    pos1 = ids1 * CAP + within1
    for b in range(BLOCKS):
        at = lax.broadcasted_iota(jnp.int32, (BROWS, tokens), 0) + b * BROWS
        hits = jnp.where(at == pos0, 1.0, 0.0) + jnp.where(at == pos1, 1.0, 0.0)
        place[b * BROWS:(b + 1) * BROWS, :] = hits.astype(BF16)

    def fill(j):
        tok_copy(j).wait()
        rows = jnp.dot(place[...], tok[j], preferred_element_type=F32)
        gz[j] = rows.astype(BF16).reshape(BLOCKS, BROWS, LANES)

    for j in FIRST_OUT:
        owned(j, lambda j=j: fill(j))

    pl.semaphore_wait(barrier, (NZ - 1) + (NY - 1) + 3)

    def z_copy(src, dst, send, recv, j, d):
        to = lax.rem(z + d, NZ)
        return push(src.at[j, to], dst.at[j, z], send.at[j, d], recv.at[j, d], to * NY + y, tp)

    def z_land(src, dst, send, recv, j, d):
        of = lax.rem(z + NZ - d, NZ)
        return push(src.at[j, of], dst.at[j, of], send.at[j, d], recv.at[j, d], ep, tp)

    def z_start(src, dst, send, recv, j):
        def one(d, _):
            z_copy(src, dst, send, recv, j, d).start()
            return 0

        lax.fori_loop(1, NZ, one, 0)
        dst[j, z] = src[j, z]

    def z_wait(src, dst, send, recv, j):
        def one(d, _):
            z_land(src, dst, send, recv, j, d).wait_recv()
            return 0

        lax.fori_loop(1, NZ, one, 0)

    def z_sent(src, dst, send, recv, j):
        def one(d, _):
            z_copy(src, dst, send, recv, j, d).wait_send()
            return 0

        lax.fori_loop(1, NZ, one, 0)

    def y_rows(at):
        return pl.ds(LOCAL * at, LOCAL)

    def as_blocks(v):
        return v.reshape(BLOCKS, BROWS, LANES)

    def as_rows(v):
        return v.reshape(ROWS, LANES)

    def quarter(q):
        return pl.ds(LOCAL * q, LOCAL)

    def half(h):
        return pl.ds(HALF * h, HALF)

    to_z = (gz, zb, zs, zr_sem)

    def y_copy(j, d):
        to = lax.rem(y + d, NY)
        return push(
            yb.at[j, y_rows(to)], xb.at[tile(x, j, c), quarter(d)], ys.at[j, d], yr_sem.at[j, d],
            z * NY + to, tp,
        )

    def x_copy(j, q, way):
        if way == 0:
            src, to = xb.at[tile(x, j, c), quarter(q)], right_id
        elif way == 1:
            src, to = xb.at[tile(x, j, c), quarter(q)], left_id
        elif q % 2 == 0:
            src, to = xb.at[tile(left, j, c), quarter(q)], right_id
        else:
            src, to = xb.at[tile(right, j, c), quarter(q)], left_id
        return push(src, src, xs.at[j, way * NY + q], xr.at[j, way * NY + q], ep, to)

    def x_land(j, q, way):
        chip = (left, right, opp)[way]
        dst = xb.at[tile(chip, j, c), quarter(q)]
        return push(dst, dst, xs.at[j, way * NY + q], xr.at[j, way * NY + q], ep, tp)

    chips = {OPP: opp, RIGHT: right, LEFT: left, OWN: x}

    def c_copy(j, h, kind):
        src = xb.at[tile(chips[kind], j, c), half(h)]
        return push(src, src, cs.at[j, 4 * h + kind], cr.at[j, 4 * h + kind], ep, twin)

    def c_land(j, h, kind):
        dst = xb.at[tile(chips[kind], j, 1 - c), half(h)]
        return push(dst, dst, cs.at[j, 4 * h + kind], cr.at[j, 4 * h + kind], ep, tp)

    def gather(j):
        if j not in FIRST_OUT:
            fill(j)
        z_start(*to_z, j)

    to_z2 = (gz2, zb2, zs2, zr2)

    def y2_copy(j, d):
        to = lax.rem(y + d, NY)
        return push(
            yb2.at[j, y_rows(to)], xb.at[tile(opp, j, c), quarter(d)], ys2.at[j, d], yr2.at[j, d],
            z * NY + to, tp,
        )

    def gather2(j):
        tok2_copy(j).wait()
        rows = jnp.dot(place[...], tok2[j], preferred_element_type=F32)
        gz2[j] = as_blocks(rows.astype(BF16))
        z_start(*to_z2, j)

    def turn2(j):
        z_wait(*to_z2, j)
        rows = jnp.dot(perm[...], as_rows(zb2[j]), preferred_element_type=F32)
        yb2[j] = as_blocks(rows.astype(BF16))
        for d in (2, 1, 3):
            y2_copy(j, d).start()
        xb[tile(opp, j, c), quarter(0)] = yb2[j, y_rows(y)]

    def spread(j, q):
        x_copy(j, q, 0).start()
        x_copy(j, q, 1).start()

    def turn(j):
        z_wait(*to_z, j)
        rows = jnp.dot(perm[...], as_rows(zb[j]), preferred_element_type=F32)
        yb[j] = as_blocks(rows.astype(BF16))
        for d in (2, 1, 3):
            y_copy(j, d).start()
        xb[tile(x, j, c), quarter(0)] = yb[j, y_rows(y)]
        spread(j, 0)

    def side(j, q):
        y_copy(j, q).wait_recv()
        spread(j, q)
        if q < 3:
            c_copy(j, q // 2, OWN).start()

    def forward(j, q):
        x_land(j, q, q % 2).wait_recv()
        if j not in OVER_Z:
            x_copy(j, q, 2).start()

    def pass_left(j, h):
        x_land(j, 2 * h + 1, 0).wait_recv()
        c_copy(j, h, LEFT).start()

    def pass_right(j, h):
        x_land(j, 2 * h, 1).wait_recv()
        c_copy(j, h, RIGHT).start()

    def last_hop(j, h):
        if j in OVER_Z:
            for d in ((1,), (2, 3))[h]:
                y2_copy(j, d).wait_recv()
        else:
            x_land(j, 2 * h, 2).wait_recv()
            x_land(j, 2 * h + 1, 2).wait_recv()
        c_copy(j, h, OPP).start()

    def multiply(j, h):
        def landed():
            for kind in (OWN, LEFT, RIGHT, OPP):
                c_land(j, h, kind).wait_recv()

        if j < FIRST - 1:
            landed()
        else:
            pl.when(c == 1)(landed)
        tiles = [chip * TILES + j for chip in range(NX)]
        if j < FIRST - 1:
            tiles += [chip * TILES + FIRST + j for chip in range(NX)]
        for e in range(LOCAL):
            rows = jnp.concatenate(
                [
                    jnp.concatenate([xb[g, LOCAL * q + e] for q in (2 * h, 2 * h + 1)], axis=0)
                    for g in tiles
                ],
                axis=1,
            )
            weight = jnp.concatenate([up[e, g * LANES:(g + 1) * LANES, :] for g in tiles], axis=0)
            product = jnp.dot(rows, weight, preferred_element_type=F32)
            if j == FIRST_UP[h]:
                raised[h, e] = product
            elif j != LAST_UP[h]:
                raised[h, e] = raised[h, e] + product
            else:
                v = raised[h, e] + product
                hid[h, e] = (v / (1.0 + jnp.exp(-v))).astype(BF16)

    def make_perm():
        for b in range(BLOCKS):
            row = lax.broadcasted_iota(jnp.int32, (BROWS, 1), 0) + b * BROWS
            block = lax.shift_right_logical(row * 205, 11)
            source = (
                (lax.bitwise_and(block, 7) * BLOCKS + lax.shift_right_logical(block, 3)) * CAP
                + row - block * CAP
            )
            column = lax.broadcasted_iota(jnp.int32, (BROWS, ROWS), 1)
            perm[b * BROWS:(b + 1) * BROWS, :] = jnp.where(column == source, 1.0, 0.0).astype(BF16)

    def make_mix():
        rw_copy.wait()
        w0, w1 = rw_ref[0:1, :], rw_ref[1:2, :]
        for b in range(BLOCKS):
            at = lax.broadcasted_iota(jnp.int32, (BROWS, tokens), 0) + b * BROWS
            mix = jnp.where(at == pos0, w0, 0.0) + jnp.where(at == pos1, w1, 0.0)
            coarse = mix.astype(BF16)
            mixw[b * BROWS:(b + 1) * BROWS, 0:tokens] = coarse
            mixw[b * BROWS:(b + 1) * BROWS, tokens:] = (mix - coarse.astype(F32)).astype(BF16)

    back_z = (zo, zr, rzs, rzr)

    def rc_copy(j, h, kind):
        src = (other if j < FIRST - 1 else part).at[j, kind, half(h)]
        at = 4 * h + kind
        return push(src, cross.at[j, kind, half(h)], rcs.at[j, at], rcr.at[j, at], ep, twin)

    def rc_land(j, h, kind):
        dst = cross.at[j, kind, half(h)]
        at = 4 * h + kind
        return push(dst, dst, rcs.at[j, at], rcr.at[j, at], ep, tp)

    def rx_copy(j, h, kind):
        if kind == 0:
            src, dst, to = part.at[j, OPP, quarter(2 * h)], half_in.at[j, h, 0], right_id
        elif kind == 1:
            src, dst, to = part.at[j, OPP, quarter(2 * h + 1)], half_in.at[j, h, 1], left_id
        elif kind == 2:
            src, dst, to = part.at[j, RIGHT, half(h)], full_in.at[j, 0, half(h)], right_id
        else:
            src, dst, to = part.at[j, LEFT, half(h)], full_in.at[j, 1, half(h)], left_id
        at = 4 * h + kind
        return push(src, dst, rxs.at[j, at], rxr.at[j, at], ep, to)

    def ry_copy(j, d):
        to = lax.rem(y + NY - d, NY)
        return push(
            summed.at[j, quarter(d)], yr.at[j, y_rows(y)], rys.at[j, d], ryr.at[j, d],
            z * NY + to, tp,
        )

    def ry_land(j, d):
        dst = yr.at[j, y_rows(lax.rem(y + d, NY))]
        return push(dst, dst, rys.at[j, d], ryr.at[j, d], ep, tp)

    def lower(j, h, kind):
        chip = chips[kind]
        for e in range(LOCAL):
            mine = down[e, :, lanes(tile(chip, j, c if j < FIRST - 1 else 0))]
            if j < FIRST - 1:
                theirs = down[e, :, lanes(tile(chip, j, 1 - c))]
                weight = jnp.concatenate([mine, theirs], axis=1)
            else:
                weight = mine
            product = jnp.dot(hid[h, e], weight, preferred_element_type=F32).astype(BF16)
            for i in range(2):
                at = LOCAL * (2 * h + i) + e
                rows = product[i * BROWS:(i + 1) * BROWS]
                if j < FIRST - 1:
                    part[j, kind, at] = rows[:, :LANES]
                    other[j, kind, at] = rows[:, LANES:]
                else:
                    part[j, kind, at] = rows
        if j < FIRST - 1:
            rc_copy(j, h, kind).start()
        else:
            pl.when(c == 1)(lambda: rc_copy(j, h, kind).start())

    def wide(v):
        return v.astype(F32)

    def add_opp(j, h):
        rc_land(j, h, OPP).wait_recv()
        at = half(h)
        part[j, OPP, at] = (wide(part[j, OPP, at]) + wide(cross[j, OPP, at])).astype(BF16)
        rx_copy(j, h, 0).start()
        rx_copy(j, h, 1).start()

    def add_side(j, h, kind):
        way = 0 if kind == RIGHT else 1
        near, far = quarter(2 * h + way), quarter(2 * h + 1 - way)
        rc_land(j, h, kind).wait_recv()
        part[j, kind, far] = (wide(part[j, kind, far]) + wide(cross[j, kind, far])).astype(BF16)
        rx_copy(j, h, way).wait_recv()
        part[j, kind, near] = (
            wide(part[j, kind, near]) + wide(cross[j, kind, near]) + wide(half_in[j, h, way])
        ).astype(BF16)
        rx_copy(j, h, 2 + way).start()

    def add_own(j, h):
        rc_land(j, h, OWN).wait_recv()
        rx_copy(j, h, 2).wait_recv()
        rx_copy(j, h, 3).wait_recv()
        at = half(h)
        summed[j, at] = (
            (wide(part[j, OWN, at]) + wide(cross[j, OWN, at]))
            + (wide(full_in[j, 0, at]) + wide(full_in[j, 1, at]))
        ).astype(BF16)
        if h == 0:
            ry_copy(j, 1).start()
            yr[j, y_rows(y)] = summed[j, quarter(0)]
        else:
            ry_copy(j, 2).start()
            ry_copy(j, 3).start()

    def turn_back(j):
        for d in (1, 2, 3):
            ry_land(j, d).wait_recv()
        rows = jnp.dot(perm[...], as_rows(yr[j]), preferred_element_type=F32)
        zo[j] = as_blocks(rows.astype(BF16))
        z_start(*back_z, j)

    mid_copy = push(mid_out, mid_in, ms, mr, ep, twin)
    middle = LANES // 2

    def mix(j):
        z_wait(*back_z, j)
        both = lax.dot_general(
            as_rows(zr[j]), mixw[...], (((0,), (0,)), ((), ())), preferred_element_type=F32
        )
        result = (both[:, :tokens] + both[:, tokens:]).astype(BF16)
        if j == FIRST - 1:
            out_ref[j * LANES:j * LANES + middle, :] = result[:middle]
            mid_out[...] = result[middle:]
            mid_copy.start()
        else:
            def first():
                out_ref[j * LANES:(j + 1) * LANES, :] = result

            def second():
                out_ref[middle + j * LANES:middle + (j + 1) * LANES, :] = result

            pl.when(c == 0)(first)
            pl.when(c == 1)(second)

    def take_middle():
        mid_copy.wait_recv()
        out_ref[0:middle, :] = mid_in[...]

    def do(step, j, *h):
        owned(j, lambda: step(j, *h))

    def all_sent(j):
        z_sent(*to_z, j)
        if j not in LATE:
            z_sent(*back_z, j)
        if j in OVER_Z:
            z_sent(*to_z2, j)
        for d in range(1, NY):
            if j in OVER_Z:
                y2_copy(j, d).wait_send()
            y_copy(j, d).wait_send()
            ry_copy(j, d).wait_send()
        for q in range(NY):
            for way in range(2 if j in OVER_Z else 3):
                x_copy(j, q, way).wait_send()
        for h in range(2):
            for kind in range(4):
                c_copy(j, h, kind).wait_send()
                rx_copy(j, h, kind).wait_send()
                if j < FIRST - 1:
                    rc_copy(j, h, kind).wait_send()

    def extras_sent():
        for h in range(2):
            for kind in range(4):
                rc_copy(FIRST - 1, h, kind).wait_send()


    do(gather, 2)
    make_perm()
    do(gather, 1)
    do(gather, 3)
    do(turn, 2)
    do(gather, 0)
    do(turn, 1)
    do(forward, 2, 0)
    do(side, 2, 1)
    do(side, 2, 3)
    do(gather2, 3)
    do(side, 2, 2)
    do(gather2, 0)
    do(turn, 3)
    do(side, 1, 1)
    do(side, 1, 3)
    do(forward, 2, 1)
    do(turn, 0)
    do(forward, 2, 2)
    do(side, 3, 1)
    do(turn2, 3)
    do(side, 3, 3)
    do(forward, 1, 0)
    do(forward, 2, 3)
    do(pass_right, 2, 0)
    do(pass_left, 2, 1)
    do(forward, 3, 0)
    do(pass_left, 2, 0)
    do(side, 1, 2)
    do(forward, 1, 1)
    do(forward, 0, 0)
    do(side, 0, 1)
    do(turn2, 0)
    do(pass_left, 3, 0)
    do(side, 0, 3)
    do(last_hop, 2, 0)
    do(pass_right, 2, 1)
    do(forward, 3, 3)
    do(side, 3, 2)
    do(forward, 3, 1)
    do(pass_right, 1, 0)
    do(last_hop, 2, 1)
    do(last_hop, 3, 0)
    do(pass_right, 3, 0)
    do(side, 0, 2)
    do(pass_left, 1, 0)
    up_copy.wait()
    multiply(2, 0)
    do(forward, 1, 3)
    do(forward, 1, 2)
    do(last_hop, 1, 0)
    multiply(2, 1)
    do(forward, 0, 1)
    do(pass_right, 1, 1)
    do(pass_right, 0, 0)
    do(pass_left, 0, 0)
    multiply(3, 0)
    do(last_hop, 0, 0)
    multiply(1, 0)
    do(forward, 3, 2)
    do(pass_left, 1, 1)
    do(pass_right, 3, 1)
    do(pass_left, 3, 1)
    do(last_hop, 3, 1)
    do(forward, 0, 3)
    do(forward, 0, 2)
    do(last_hop, 0, 1)
    do(pass_right, 0, 1)
    do(pass_left, 0, 1)
    multiply(0, 0)
    down_copy.wait()
    lower(0, 0, OPP)
    lower(2, 0, OPP)
    lower(1, 0, OPP)
    do(last_hop, 1, 1)
    multiply(3, 1)
    do(add_opp, 0, 0)
    multiply(0, 1)
    do(add_opp, 1, 0)
    multiply(1, 1)
    lower(0, 1, OPP)
    do(add_opp, 2, 0)
    lower(3, 1, RIGHT)
    lower(3, 1, OPP)
    lower(3, 0, OPP)
    lower(0, 0, LEFT)
    do(add_opp, 0, 1)
    lower(0, 0, RIGHT)
    lower(0, 0, OWN)
    do(add_opp, 3, 1)
    lower(1, 0, RIGHT)
    lower(0, 1, LEFT)
    do(add_opp, 3, 0)
    lower(0, 1, RIGHT)
    do(add_side, 0, 0, LEFT)
    lower(2, 1, OPP)
    do(add_side, 0, 0, RIGHT)
    lower(0, 1, OWN)
    lower(3, 1, LEFT)
    lower(1, 1, OPP)
    lower(2, 1, OWN)
    do(add_side, 0, 1, LEFT)
    do(add_side, 0, 1, RIGHT)
    lower(2, 1, LEFT)
    do(add_opp, 1, 1)
    do(add_opp, 2, 1)
    lower(2, 0, LEFT)
    lower(2, 1, RIGHT)
    lower(3, 0, LEFT)
    lower(1, 1, RIGHT)
    lower(2, 0, RIGHT)
    lower(3, 0, OWN)
    lower(1, 0, LEFT)
    lower(1, 1, LEFT)
    lower(3, 0, RIGHT)
    lower(3, 1, OWN)
    do(add_side, 3, 1, LEFT)
    lower(1, 0, OWN)
    do(add_side, 3, 1, RIGHT)
    lower(1, 1, OWN)
    do(add_side, 3, 0, LEFT)
    do(add_side, 3, 0, RIGHT)
    do(add_own, 0, 1)
    do(add_own, 0, 0)
    do(add_side, 1, 1, LEFT)
    do(add_side, 1, 0, LEFT)
    do(add_side, 1, 1, RIGHT)
    lower(2, 0, OWN)
    do(add_side, 1, 0, RIGHT)
    do(add_side, 2, 1, RIGHT)
    do(add_own, 3, 1)
    make_mix()
    do(add_side, 2, 0, RIGHT)
    do(add_own, 3, 0)
    do(add_side, 2, 1, LEFT)
    do(add_side, 2, 0, LEFT)
    do(turn_back, 0)
    do(turn_back, 3)
    do(add_own, 1, 1)
    do(add_own, 1, 0)
    do(add_own, 2, 1)
    do(add_own, 2, 0)
    do(turn_back, 1)
    do(mix, 3)
    do(mix, 0)
    do(turn_back, 2)
    pl.when(c == 1)(take_middle)
    do(mix, 1)
    for j in range(FIRST):
        do(all_sent, j)
    pl.when(c == 1)(extras_sent)
    do(mix, 2)

    for j in LATE:
        do(lambda j: z_sent(*back_z, j), j)
    pl.when(c == 0)(lambda: mid_copy.wait_send())


def on_device(tokens, expert_ids, routing_weights, up_weight, down_weight):
    count, width = tokens.shape
    hidden = up_weight.shape[2]
    dma = pltpu.SemaphoreType.DMA
    blocks = (BLOCKS, BROWS, LANES)
    any_space = pl.BlockSpec(memory_space=pl.ANY)
    in_vmem = pl.BlockSpec(memory_space=pltpu.VMEM)
    per_z, per_y = dma((FIRST, NZ)), dma((FIRST, NY))
    by_way, by_kind = dma((FIRST, 3 * NY)), dma((FIRST, 8))
    tile_set = pltpu.VMEM((FIRST,) + blocks, BF16)
    kind_set = pltpu.VMEM((FIRST, 4) + blocks, BF16)
    return pl.pallas_call(
        kernel,
        out_shape=jax.ShapeDtypeStruct((width // (NX * NC), count), BF16),
        in_specs=[any_space] * 5,
        out_specs=in_vmem,
        scratch_shapes=[
            pltpu.VMEM((TOP, count), jnp.int32),
            pltpu.VMEM((TOP, count), F32),
            pltpu.VMEM((FIRST, count, LANES), BF16),
            pltpu.VMEM(up_weight.shape, BF16),
            pltpu.VMEM(down_weight.shape, BF16),
            pltpu.VMEM((ROWS, count), BF16),
            pltpu.VMEM((ROWS, ROWS), BF16),
            pltpu.VMEM((ROWS, 2 * count), BF16),
            pltpu.VMEM((FIRST, count, LANES), BF16),
            tile_set,
            tile_set,
            tile_set,
            tile_set,
            tile_set,
            tile_set,
            pltpu.VMEM((NX * TILES,) + blocks, BF16),
            pltpu.VMEM((2, LOCAL, ROWS // LOCAL // 2, hidden), F32),
            pltpu.VMEM((2, LOCAL, ROWS // LOCAL // 2, hidden), BF16),
            kind_set,
            pltpu.VMEM((FIRST - 1, 4) + blocks, BF16),
            kind_set,
            pltpu.VMEM((FIRST, 2, 2, LOCAL, BROWS, LANES), BF16),
            pltpu.VMEM((FIRST, 2) + blocks, BF16),
            tile_set,
            tile_set,
            tile_set,
            tile_set,
            pltpu.VMEM((LANES // 2, count), BF16),
            pltpu.VMEM((LANES // 2, count), BF16),
            dma((FIRST,)),
            dma((4,)),
            dma((FIRST,)), per_z, per_z, per_y, per_y,
            per_z, per_z, per_y, per_y, by_way, by_way, by_kind, by_kind,
            by_kind, by_kind, by_kind, by_kind, per_y, per_y, per_z, per_z, dma, dma,
        ],
        compiler_params=pltpu.CompilerParams(
            collective_id=0, has_side_effects=True, vmem_limit_bytes=52 * 1024 * 1024
        ),
        cost_estimate=pl.CostEstimate(
            flops=4 * ROWS * width * hidden, bytes_accessed=8 * width * hidden, transcendentals=0
        ),
        name="experts",
    )(expert_ids.T, routing_weights.T, tokens, up_weight, down_weight).T


def solution(mesh):
    placed = (P("ep", None), P("ep", None), P("ep", None), P("ep", None, "tp"), P("ep", "tp", None))
    return jax.shard_map(
        on_device, mesh=mesh, in_specs=placed, out_specs=P("ep", "tp"), check_vma=False
    )
```
